512 devices in a mesh: row: 32 (over y, z_lo, core), col: 16 (over x, z_hi).
Axes of the slice: x: 4, y: 4, z: 16 (z_hi: 4, z_lo: 4; z = z_hi * 4 + z_lo), core: 2. Of those that a mesh axis runs over, the one named last changes fastest.
Arguments:
- pair_map: bfloat16 [256, 256, 128], P('row', 'col'), may hold values from -6 to 6
- out_proj: bfloat16 [128, 512], replicated, may hold values from -0.5 to 0.5
- out_gate: bfloat16 [128, 128], replicated, may hold values from -0.5 to 0.5
- out_final: bfloat16 [128, 128], replicated, may hold values from -0.5 to 0.5
- in_proj: bfloat16 [128, 512], replicated, may hold values from -0.5 to 0.5
- in_gate: bfloat16 [128, 128], replicated, may hold values from -0.5 to 0.5
- in_final: bfloat16 [128, 128], replicated, may hold values from -0.5 to 0.5
Outputs:
- updated_map: bfloat16 [256, 256, 128], P('row', 'col')
The draws below stay inside these ranges and needn't reach their ends.
All inputs are finite; a program needn't handle non-finite values.
Results may differ from the reference program's by a relative error of at most 0.015.
Values may be sent and summed in bfloat16 or wider, within the bound.
A program may use at most 64 MiB of HBM per device.

```python
import jax
import jax.numpy as jnp
from jax import lax

C = 128
H = 128
TOKENS = 256


def block_scale(stream_key, dims, pieces, least, top_value):
    def one(position, blocks):
        steps = jax.random.uniform(jax.random.fold_in(jax.random.fold_in(stream_key, 6), position), (blocks,), jnp.float32, least / len(pieces), top_value / len(pieces))
        return jnp.repeat(jnp.exp(steps), dims[position] // blocks).reshape((-1,) + (1,) * (len(dims) - position - 1))

    factor_of = one(*pieces[0])
    for cut in pieces[1:]:
        factor_of = factor_of * one(*cut)
    return factor_of


def normal_values(stream_key, shape, scale, bound, pieces=(), kind=jnp.bfloat16):
    gain = block_scale(stream_key, shape, pieces, -0.22, 0.18) if pieces else 1.0
    drawn = jax.random.normal(stream_key, shape, jnp.float32) * scale * gain
    return jnp.minimum(jnp.maximum(drawn, -bound), bound).astype(kind)


def setup_inputs(seed: int = 0) -> dict:
    splits = jax.random.split(jax.random.key(seed), 8)
    pair_map = normal_values(splits[0], (TOKENS, TOKENS, C), 1.0, 6.0, ((0, 32), (1, 16)))
    out_proj = normal_values(splits[1], (C, 4 * H), C ** -0.5, 0.5)
    out_gate = normal_values(splits[2], (C, C), C ** -0.5, 0.5)
    out_final = normal_values(splits[3], (H, C), H ** -0.5, 0.5)
    in_proj = normal_values(splits[4], (C, 4 * H), C ** -0.5, 0.5)
    in_gate = normal_values(splits[5], (C, C), C ** -0.5, 0.5)
    in_final = normal_values(splits[6], (H, C), H ** -0.5, 0.5)
    return {"pair_map": pair_map, "out_proj": out_proj, "out_gate": out_gate, "out_final": out_final, "in_proj": in_proj, "in_gate": in_gate, "in_final": in_final}


def normalize(values):
    average = lax.optimization_barrier(jnp.mean(values, axis=-1, keepdims=True))
    centred = values - average
    spread = lax.optimization_barrier(jnp.mean(centred * centred, axis=-1, keepdims=True))
    return centred * jax.lax.rsqrt(spread + 1e-05)

def triangle(pair_map, w_proj, w_gate, w_final, incoming):
    hidden = w_final.shape[0]
    normed = normalize(pair_map.astype(jnp.float32)).astype(jnp.bfloat16)
    projected = jnp.dot(normed, w_proj, preferred_element_type=jnp.float32)
    left_side = (jax.nn.sigmoid(projected[..., 0:hidden]) * projected[..., hidden:2 * hidden]).astype(jnp.bfloat16)
    right_side = (jax.nn.sigmoid(projected[..., 2 * hidden:3 * hidden]) * projected[..., 3 * hidden:]).astype(jnp.bfloat16)
    gate_vals = jax.nn.sigmoid(jnp.dot(normed, w_gate, preferred_element_type=jnp.float32))
    if incoming:
        summed = jnp.einsum('kih,kjh->ijh', left_side.astype(jnp.float32), right_side.astype(jnp.float32))
    else:
        summed = jnp.einsum('ikh,jkh->ijh', left_side.astype(jnp.float32), right_side.astype(jnp.float32))
    mixed_norm = normalize(summed).astype(jnp.bfloat16)
    update = gate_vals * jnp.dot(mixed_norm, w_final, preferred_element_type=jnp.float32)
    return (pair_map.astype(jnp.float32) + update).astype(jnp.bfloat16)

def reference(pair_map, out_proj, out_gate, out_final, in_proj, in_gate, in_final):
    after_out = triangle(pair_map, out_proj, out_gate, out_final, False)
    return triangle(after_out, in_proj, in_gate, in_final, True)
```

```python
import functools

import jax
import jax.numpy as jnp
from jax import lax
from jax.experimental import pallas as pl
from jax.experimental.pallas import tpu as pltpu
from jax.sharding import PartitionSpec as P

MESH = pl.DeviceIdType.MESH
F32 = jnp.float32
BF16 = jnp.bfloat16


def normalize(values):
    average = jnp.mean(values, axis=-1, keepdims=True)
    centred = values - average
    spread = jnp.mean(centred * centred, axis=-1, keepdims=True)
    return centred * lax.rsqrt(spread + 1e-05)


def prepare(block, proj_ref, gate_ref):
    normed = normalize(block.astype(F32)).astype(BF16)
    projected = jnp.dot(normed, proj_ref[...], preferred_element_type=F32)
    left = jax.nn.sigmoid(projected[:, 0:128]) * projected[:, 128:256]
    right = jax.nn.sigmoid(projected[:, 256:384]) * projected[:, 384:512]
    gate = jax.nn.sigmoid(jnp.dot(normed, gate_ref[...], preferred_element_type=F32))
    return left, right, gate


def finish(block, summed, gate, final_ref):
    mixed = normalize(summed).astype(BF16)
    update = gate * jnp.dot(mixed, final_ref[...], preferred_element_type=F32)
    return (block.astype(F32) + update).astype(BF16)


def contract(left, right, sums, half):
    for i_block in range(2):
        for j_half in range(2):

            def step(chunk, total):
                a = left[chunk, half, i_block * 32 : i_block * 32 + 32, :].astype(F32)
                b = right[chunk, j_half].astype(F32)
                return total + a.reshape(4, 1, 8, 128) * b.reshape(1, 8, 8, 128)

            total = lax.fori_loop(0, 16, step, jnp.zeros((4, 8, 8, 128), F32))
            sums[half, i_block * 4 : i_block * 4 + 4, j_half * 8 : j_half * 8 + 8, :] = (
                jnp.sum(total, axis=2)
            )


def kernel(
    map_ref, proj1, gate1, final1, proj2, gate2, final2, out_ref,
    send_l1, send_r1, send_l2, send_r2, left1, right1, left2, right2, sums1, sums2, part1, part2, turned,
    out_a_l1, in_a_l1, out_b_l1, in_b_l1, out_a_r1, in_a_r1, out_b_r1, in_b_r1,
    out_a_l2, in_a_l2, out_b_l2, in_b_l2, out_a_r2, in_a_r2, out_b_r2, in_b_r2,
    out_part, in_part,
):
    row, col = lax.axis_index("row"), lax.axis_index("col")
    y, zl, core = row // 8, row // 2 % 4, row % 2
    x, zh = col // 4, col % 4

    def at(x_, y_, zh_, zl_, core_):
        return (y_ * 8 + zl_ * 2 + core_, x_ * 4 + zh_)

    def plus(value, step):
        return (value + step) % 4

    own_turn = jnp.logical_and(x == y, zh == zl)
    other_turn = jnp.logical_not(own_turn)
    sibling = at(x, y, zh, zl, 1 - core)
    pending = []

    def copy(src, dst, send, recv, device):
        return pltpu.make_async_remote_copy(
            src_ref=src, dst_ref=dst, send_sem=send, recv_sem=recv, device_id=device, device_id_type=MESH
        )

    def push(src, dst, send, recv, device):
        c = copy(src, dst, send, recv, device)
        c.start()
        pending.append(c)

    def landed(dst, recv):
        copy(dst, dst, out_part.at[0], recv, sibling).wait_recv()

    def turn_push(src, dst, send, recv, device):
        c = copy(src, dst, send, recv, device)

        @pl.when(other_turn)
        def _():
            c.start()

        @pl.when(own_turn)
        def _():
            pltpu.make_async_copy(src, dst, recv).start()

        return c

    barrier = pltpu.get_barrier_semaphore()

    def greet(device):
        pl.semaphore_signal(barrier, inc=1, device_id=device, device_id_type=MESH)

    greeted = 0
    for step in range(4):
        for side in range(2):
            c_ = (core + side) % 2
            for device in (
                at(y, x, zl, plus(zl, step), c_),
                at(y, x, plus(zh, step), zh, c_),
            ):
                if step or side:
                    greet(device)
                else:

                    @pl.when(other_turn)
                    def _(device=device):
                        greet(device)

                greeted += 1
            if step or side:
                greet(at(x, y, plus(zh, step), zl, c_))
                greeted += 1
        if step:
            greet(at(plus(x, step), y, zh, zl, core))
            greet(at(x, plus(y, step), zh, zl, core))
            greet(at(x, y, zh, plus(zl, step), core))
            greeted += 3

    block = map_ref[...].reshape(128, 128)
    left, right, gate = prepare(block, proj1, gate1)
    left, right = left.reshape(8, 2, 8, 128), right.reshape(8, 2, 8, 128)
    for side in range(2):
        send_l1[side] = left[:, side].reshape(64, 128).astype(BF16)
        send_r1[side] = right[:, side].reshape(64, 128).astype(BF16)
    mine = 4 * x + zh
    left1[mine, core] = send_l1[core]

    pl.semaphore_wait(barrier, greeted - 2 * own_turn.astype(jnp.int32))

    order = (2, 1, 3, 0)
    for step in order:
        for side in (0, 1):
            to = (core + side) % 2
            if step or side:
                push(send_l1.at[to], left1.at[mine, core], out_a_l1.at[step, side], in_a_l1.at[step, side],
                     at(x, y, plus(zh, step), zl, to))
            src, dst = send_r1.at[to], right1.at[mine, core]
            send, recv = out_a_r1.at[step, side], in_a_r1.at[zh, core]
            device = at(y, x, zl, plus(zl, step), to)
            if step or side:
                push(src, dst, send, recv, device)
            else:
                turn1 = turn_push(src, dst, send, recv, device)

    for step in (0, 1, 3, 2):
        from_zh = (zh + 4 - step) % 4
        chunk = 4 * x + from_zh
        for side in (0, 1):
            if step or side:
                landed(left1.at[chunk, (core + side) % 2], in_a_l1.at[step, side])
        for hop in (2, 1, 3):
            push(left1.at[chunk], left1.at[chunk], out_b_l1.at[hop, step], in_b_l1.at[hop, step],
                 at(plus(x, hop), y, zh, zl, core))
        chunk = 4 * y + from_zh
        for side in (0, 1):
            landed(right1.at[chunk, side], in_a_r1.at[from_zh, side])
        for hop in (2, 1, 3):
            push(right1.at[chunk], right1.at[chunk], out_b_r1.at[hop, step], in_b_r1.at[hop, from_zh],
                 at(x, plus(y, hop), zh, zl, core))
    for step in (0, 1, 3, 2):
        from_zh = (zh + 4 - step) % 4
        for hop in (1, 3, 2):
            landed(left1.at[4 * ((x + 4 - hop) % 4) + from_zh], in_b_l1.at[hop, step])
            landed(right1.at[4 * ((y + 4 - hop) % 4) + from_zh], in_b_r1.at[hop, from_zh])

    contract(left1, right1, sums1, 1 - core)
    push(sums1.at[1 - core], part1, out_part.at[0], in_part.at[0], sibling)
    contract(left1, right1, sums1, core)
    landed(part1, in_part.at[0])
    summed = (sums1[core] + part1[...]).reshape(128, 128)
    block = finish(block, summed, gate, final1)

    left, right, gate = prepare(block, proj2, gate2)
    turned[0] = left
    turned[1] = right
    for j in range(0, 16, 2):
        for which, send_ref in ((0, send_l2), (1, send_r2)):
            pair = [turned[which, pl.ds(j + k, 8, stride=16), :] for k in range(2)]
            send_ref[j // 8, (j % 8) * 8 : (j % 8) * 8 + 16, :] = jnp.concatenate(pair, axis=0).astype(BF16)
    mine = 4 * y + zl
    right2[mine] = send_r2[...]
    for step in order:
        src, dst = send_l2, left2.at[mine]
        send, recv = out_a_l2.at[step], in_a_l2.at[zl]
        device = at(y, x, plus(zh, step), zh, core)
        if step:
            push(src, dst, send, recv, device)
            push(send_r2, right2.at[mine], out_a_r2.at[step], in_a_r2.at[step], at(x, y, zh, plus(zl, step), core))
        else:
            turn2 = turn_push(src, dst, send, recv, device)

    for step in (0, 1, 3, 2):
        from_zl = (zl + 4 - step) % 4
        chunk = 4 * y + from_zl
        if step:
            landed(right2.at[chunk], in_a_r2.at[step])
        for hop in (2, 1, 3):
            push(right2.at[chunk], right2.at[chunk], out_b_r2.at[hop, step], in_b_r2.at[hop, step],
                 at(x, plus(y, hop), zh, zl, core))
        chunk = 4 * x + from_zl
        landed(left2.at[chunk], in_a_l2.at[from_zl])
        for hop in (2, 1, 3):
            push(left2.at[chunk], left2.at[chunk], out_b_l2.at[hop, step], in_b_l2.at[hop, from_zl],
                 at(plus(x, hop), y, zh, zl, core))
    for step in (0, 1, 3, 2):
        from_zl = (zl + 4 - step) % 4
        for hop in (1, 3, 2):
            landed(right2.at[4 * ((y + 4 - hop) % 4) + from_zl], in_b_r2.at[hop, step])
            landed(left2.at[4 * ((x + 4 - hop) % 4) + from_zl], in_b_l2.at[hop, from_zl])

    contract(left2, right2, sums2, 1 - core)
    push(sums2.at[1 - core], part2, out_part.at[1], in_part.at[1], sibling)
    contract(left2, right2, sums2, core)
    landed(part2, in_part.at[1])
    summed = (sums2[core] + part2[...]).reshape(128, 128)
    out_ref[...] = finish(block, summed, gate, final2).reshape(8, 16, 128)

    for c in pending:
        c.wait_send()

    @pl.when(other_turn)
    def _():
        turn1.wait_send()
        turn2.wait_send()


def body(*args):
    vmem = pl.BlockSpec(memory_space=pltpu.VMEM)
    dma = pltpu.SemaphoreType.DMA
    half = pltpu.VMEM((2, 64, 128), BF16)
    gathered = pltpu.VMEM((16, 2, 64, 128), BF16)
    return pl.pallas_call(
        kernel,
        out_shape=jax.ShapeDtypeStruct((8, 16, 128), BF16),
        in_specs=[vmem] * 7,
        out_specs=vmem,
        scratch_shapes=[half] * 4
        + [gathered] * 4
        + [pltpu.VMEM((2, 8, 16, 128), F32)] * 2
        + [pltpu.VMEM((8, 16, 128), F32)] * 2
        + [pltpu.VMEM((2, 128, 128), F32)]
        + [dma((4, 2))] * 2 + [dma((4, 4))] * 2
        + [dma((4, 2))] * 2 + [dma((4, 4))] * 2
        + [dma((4,))] * 2 + [dma((4, 4))] * 2
        + [dma((4,))] * 2 + [dma((4, 4))] * 2
        + [dma((2,))] * 2,
        compiler_params=pltpu.CompilerParams(
            collective_id=0, has_side_effects=True, vmem_limit_bytes=32 * 1024 * 1024
        ),
        name="triangles",
    )(*args)


def solution(mesh):
    return jax.shard_map(
        body,
        mesh=mesh,
        in_specs=(P("row", "col", None), P(), P(), P(), P(), P(), P()),
        out_specs=P("row", "col", None),
        check_vma=False,
    )
```

```python
import jax
import jax.numpy as jnp
from jax import lax
from jax.experimental import pallas as pl
from jax.experimental.pallas import tpu as pltpu
from jax.sharding import PartitionSpec as P

MESH = pl.DeviceIdType.MESH
F32 = jnp.float32
BF16 = jnp.bfloat16


def normalize(values):
    average = jnp.mean(values, axis=-1, keepdims=True)
    centred = values - average
    spread = jnp.mean(centred * centred, axis=-1, keepdims=True)
    return centred * lax.rsqrt(spread + 1e-05)


def prepare(block, proj_ref):
    normed = normalize(block.astype(F32)).astype(BF16)
    projected = jnp.dot(normed, proj_ref[...], preferred_element_type=F32)
    left = jax.nn.sigmoid(projected[:, 0:128]) * projected[:, 128:256]
    right = jax.nn.sigmoid(projected[:, 256:384]) * projected[:, 384:512]
    return left, right


def output_gate(block, gate_ref):
    normed = normalize(block.astype(F32)).astype(BF16)
    return jax.nn.sigmoid(jnp.dot(normed, gate_ref[...], preferred_element_type=F32))


def finish(block, summed, gate, final_ref):
    mixed = normalize(summed).astype(BF16)
    update = gate * jnp.dot(mixed, final_ref[...], preferred_element_type=F32)
    return (block.astype(F32) + update).astype(BF16)


def outer(a, b):
    a, b = a.astype(F32), b.astype(F32)
    i, j, k = 4, 8, a.shape[0] // 32
    a, b = a.reshape(i, k, 8, 128), b.reshape(j, k, 8, 128)
    total = None
    for n in range(k):
        term = a[:, None, n] * b[None, :, n]
        total = term if total is None else total + term
    return total


def kernel(
    map_in, proj1_in, gate1_in, final1_in, proj2_in, gate2_in, final2_in, out_ref,
    map_ref, proj1, gate1, final1, proj2, gate2, final2, load,
    send_l1, send_r1, left1, right1, send_p1, part1, own1, block1, middle,
    turned, send_l2, send_r2, left2, right2, total2, sums2, part2, block2,
    out_l1, in_l1, out_a_r1, in_a_r1, out_b_r1, in_b_r1, out_p1, in_p1, out_z, in_z,
    out_a_l2, in_a_l2, out_b_l2, in_b_l2, out_a_r2, in_a_r2, out_b_r2, in_b_r2, out_p2, in_p2,
):
    row, col = lax.axis_index("row"), lax.axis_index("col")
    y, zl, core = row // 8, row // 2 % 4, row % 2
    x, zh = col // 4, col % 4

    def at(x_, y_, zh_, zl_, core_):
        return (y_ * 8 + zl_ * 2 + core_, x_ * 4 + zh_)

    def plus(value, step):
        return (value + step) % 4

    def minus(value, step):
        return (value + 4 - step) % 4

    flat, level = x == y, zl == zh
    sibling = at(x, y, zh, zl, 1 - core)
    swapped = at(y, x, zh, zl, core)
    pending, turns = [], []

    def copy(src, dst, send, recv, device):
        return pltpu.make_async_remote_copy(
            src_ref=src, dst_ref=dst, send_sem=send, recv_sem=recv, device_id=device, device_id_type=MESH
        )

    def push(src, dst, send, recv, device):
        c = copy(src, dst, send, recv, device)
        c.start()
        pending.append(c)

    def push_unless(stays, src, dst, send, recv, device):
        c = copy(src, dst, send, recv, device)

        @pl.when(jnp.logical_not(stays))
        def _():
            c.start()

        @pl.when(stays)
        def _():
            pltpu.make_async_copy(src, dst, recv).start()

        turns.append((stays, c))

    def landed(dst, recv):
        copy(dst, dst, out_p2.at[0], recv, sibling).wait_recv()

    loads = [
        pltpu.make_async_copy(src, dst, load.at[n])
        for n, (src, dst) in enumerate((
            (map_in, map_ref), (proj1_in, proj1), (gate1_in, gate1), (final1_in, final1),
            (proj2_in, proj2), (gate2_in, gate2), (final2_in, final2),
        ))
    ]
    for c in loads:
        c.start()

    barrier = pltpu.get_barrier_semaphore()
    greeted = []

    def greet(device, stays=None):
        def signal():
            pl.semaphore_signal(barrier, inc=1, device_id=device, device_id_type=MESH)

        if stays is None:
            signal()
            greeted.append(1)
        else:
            pl.when(jnp.logical_not(stays))(signal)
            greeted.append(1 - stays.astype(jnp.int32))

    for step in (2, 1, 3, 0):
        for side in (0, 1):
            other = (core + side) % 2
            home = None if step or side else flat
            if step or side:
                greet(at(x, y, plus(zh, step), zl, other))
            greet(at(y, plus(y, step), zh, zl, other), home)
            greet(at(plus(x, step), x, zh, zl, other), home)
        home = None if step else level
        greet(at(x, y, plus(zh, step), zh, core), home)
        greet(at(x, y, zl, plus(zl, step), core), home)
        greet(at(y, x, zh, plus(zl, step), core), None if step else flat)
        if step:
            greet(at(plus(x, step), y, zh, zl, core))
            greet(at(x, plus(y, step), zh, zl, core))
            greet(at(x, y, zh, plus(zl, step), core))

    for c in loads[:2]:
        c.wait()
    left, right = prepare(map_ref[...].reshape(128, 128), proj1)
    send_r1[...] = right.astype(BF16)
    right1[x, zl] = send_r1[...]
    send_l1[...] = left.astype(BF16)

    pl.semaphore_wait(barrier, sum(greeted))

    for step in (2, 1, 3):
        push(send_r1, right1.at[x, zl], out_a_r1.at[step], in_a_r1.at[zl], at(x, y, zh, plus(zl, step), core))
    for step in (2, 1, 3, 0):
        for side in (1, 0):
            device = at(y, plus(y, step), zh, zl, (core + side) % 2)
            args = send_l1, left1.at[x, core], out_l1.at[step, side], in_l1.at[x, core], device
            if step or side:
                push(*args)
            else:
                push_unless(flat, *args)
    for step in (0, 1, 3, 2):
        from_zl = minus(zl, step)
        piece = right1.at[x, from_zl]
        if step:
            landed(piece, in_a_r1.at[from_zl])
        for hop in (2, 1, 3):
            push(piece, piece, out_b_r1.at[hop, step], in_b_r1.at[x, from_zl], at(plus(x, hop), y, zh, zl, core))
    push_unless(flat, map_ref, block1, out_z.at[0], in_z.at[0], swapped)

    for from_x in range(4):
        for side in range(2):
            landed(left1.at[from_x, side], in_l1.at[from_x, side])
    for step in (2, 1, 3, 0):
        to_zh = plus(zh, step)
        for hop in (1, 3, 2):
            landed(right1.at[minus(x, hop), to_zh], in_b_r1.at[minus(x, hop), to_zh])

        def four_rows(n, _, step=step, to_zh=to_zh):
            half, quarter = n // 2, n % 2
            total = None
            for from_x in range(4):
                term = outer(
                    left1[from_x, half, pl.ds(pl.multiple_of(quarter * 64, 64), 64), :], right1[from_x, to_zh]
                )
                total = term if total is None else total + term
            part = jnp.sum(total, axis=2).reshape(32, 128)
            rows = pl.ds(pl.multiple_of(quarter * 32, 32), 32)
            send_p1[step, half, rows, :] = part.astype(BF16)
            if step == 0:
                own1[half, rows, :] = part
            return 0

        lax.fori_loop(0, 4, four_rows, 0)
        for side in (0, 1):
            to = (core + side) % 2
            if step or side:
                push(send_p1.at[step, to], part1.at[step, core], out_p1.at[step, side], in_p1.at[step, core],
                     at(x, y, to_zh, zl, to))

    landed(block1, in_z.at[0])
    for c in loads[2:]:
        c.wait()
    block = block1[...].reshape(128, 128)
    gate = output_gate(block, gate1)
    landed(part1.at[0, 1 - core], in_p1.at[0, 1 - core])
    for step in (1, 3, 2):
        for side in (0, 1):
            landed(part1.at[step, side], in_p1.at[step, side])
    halves = []
    for side in range(2):
        near = jnp.where(core == side, own1[side], part1[0, side].astype(F32))
        rest = part1[1, side].astype(F32) + part1[2, side].astype(F32) + part1[3, side].astype(F32)
        halves.append((near + rest).reshape(8, 1, 8, 128))
    summed = jnp.concatenate(halves, axis=1).reshape(128, 128)
    block = finish(block, summed, gate, final1)
    middle[...] = block.reshape(8, 16, 128)

    left, right = prepare(block, proj2)
    turned[0] = left
    turned[1] = right
    for which, send_ref in ((0, send_l2), (1, send_r2)):
        for j in range(0, 16, 2):
            pair = [turned[which, pl.ds(j + k, 8, stride=16), :] for k in range(2)]
            send_ref[j // 8, (j % 8) * 8 : (j % 8) * 8 + 16, :] = jnp.concatenate(pair, axis=0).astype(BF16)
    for step in (2, 1, 3, 0):
        args = send_l2, left2.at[x, zl], out_a_l2.at[step], in_a_l2.at[zl], at(x, y, plus(zh, step), zh, core)
        if step:
            push(*args)
        else:
            push_unless(level, *args)
        args = send_r2, right2.at[x, zl], out_a_r2.at[step], in_a_r2.at[zl], at(y, x, zh, plus(zl, step), core)
        if step:
            push(*args)
        else:
            push_unless(flat, *args)
    push_unless(flat, middle, block2, out_z.at[1], in_z.at[1], swapped)

    for step in (0, 1, 3, 2):
        from_zl = minus(zl, step)
        piece = right2.at[y, from_zl]
        landed(piece, in_a_r2.at[from_zl])
        for hop in (2, 1, 3):
            push(piece, piece, out_b_r2.at[hop, step], in_b_r2.at[y, from_zl], at(x, plus(y, hop), zh, zl, core))
        piece = left2.at[x, from_zl]
        landed(piece, in_a_l2.at[from_zl])
        for hop in (2, 1, 3):
            push(piece, piece, out_b_l2.at[hop, step], in_b_l2.at[x, from_zl], at(plus(x, hop), y, zh, zl, core))

    landed(block2, in_z.at[1])
    block = block2[...].reshape(128, 128)
    gate = output_gate(block, gate2)
    for step in (0, 1, 3, 2):
        from_zl = minus(zl, step)
        for hop in (1, 3, 2):
            landed(right2.at[minus(y, hop), from_zl], in_b_r2.at[minus(y, hop), from_zl])
            landed(left2.at[minus(x, hop), from_zl], in_b_l2.at[minus(x, hop), from_zl])

        def four_by_eight(n, _, step=step, from_zl=from_zl):
            half, quarter, j_half = n // 4, n // 2 % 2, n % 2
            total = None if step == 0 else total2[n]
            for from_x in range(4):
                term = outer(
                    left2[from_x, from_zl, half, pl.ds(pl.multiple_of(quarter * 32, 32), 32), :],
                    right2[from_x, from_zl, j_half],
                )
                total = term if total is None else total + term
            if step == 2:
                sums2[half, quarter, :, j_half] = jnp.sum(total, axis=2)
            else:
                total2[n] = total
            return 0

        if step == 2:
            first = (1 - core) * 4
            lax.fori_loop(first, first + 4, four_by_eight, 0)
            push(sums2.at[1 - core], part2, out_p2.at[0], in_p2.at[0], sibling)
            first = core * 4
            lax.fori_loop(first, first + 4, four_by_eight, 0)
        else:
            lax.fori_loop(0, 8, four_by_eight, 0)

    landed(part2, in_p2.at[0])
    summed = (sums2[core] + part2[...]).reshape(128, 128)
    out_ref[...] = finish(block, summed, gate, final2).reshape(8, 16, 128)

    for c in pending:
        c.wait_send()
    for stays, c in turns:
        pl.when(jnp.logical_not(stays))(c.wait_send)


def body(*args):
    dma = pltpu.SemaphoreType.DMA
    weights = [pltpu.VMEM((128, 512), BF16), pltpu.VMEM((128, 128), BF16), pltpu.VMEM((128, 128), BF16)]
    tile = pltpu.VMEM((8, 16, 128), BF16)
    return pl.pallas_call(
        kernel,
        out_shape=jax.ShapeDtypeStruct((8, 16, 128), BF16),
        in_specs=[pl.BlockSpec(memory_space=pl.ANY)] * 7,
        out_specs=pl.BlockSpec(memory_space=pltpu.VMEM),
        scratch_shapes=[tile, *weights, *weights, dma((7,))]
        + [pltpu.VMEM((128, 128), BF16)] * 2
        + [pltpu.VMEM((4, 2, 128, 128), BF16), pltpu.VMEM((4, 4, 128, 128), BF16)]
        + [pltpu.VMEM((4, 2, 64, 128), BF16)] * 2
        + [pltpu.VMEM((2, 64, 128), F32), tile, tile]
        + [pltpu.VMEM((2, 128, 128), F32)]
        + [pltpu.VMEM((2, 64, 128), BF16)] * 2
        + [pltpu.VMEM((4, 4, 2, 64, 128), BF16)] * 2
        + [pltpu.VMEM((8, 4, 8, 8, 128), F32), pltpu.VMEM((2, 2, 4, 2, 8, 128), F32)]
        + [pltpu.VMEM((2, 4, 2, 8, 128), F32), tile]
        + [dma((4, 2))] * 2 + [dma((4,))] * 2 + [dma((4, 4))] * 2 + [dma((4, 2))] * 2 + [dma((2,))] * 2
        + [dma((4,))] * 2 + [dma((4, 4))] * 2 + [dma((4,))] * 2 + [dma((4, 4))] * 2 + [dma((1,))] * 2,
        compiler_params=pltpu.CompilerParams(
            collective_id=0, has_side_effects=True, vmem_limit_bytes=64 * 1024 * 1024 - 65536
        ),
        name="triangles",
    )(*args)


def solution(mesh):
    return jax.shard_map(
        body,
        mesh=mesh,
        in_specs=(P("row", "col", None), P(), P(), P(), P(), P(), P()),
        out_specs=P("row", "col", None),
        check_vma=False,
    )
```

```python
import jax
import jax.numpy as jnp
from jax import lax
from jax.experimental import pallas as pl
from jax.experimental.pallas import tpu as pltpu
from jax.sharding import PartitionSpec as P

MESH = pl.DeviceIdType.MESH
F32 = jnp.float32
BF16 = jnp.bfloat16


def normalize(values):
    average = jnp.mean(values, axis=-1, keepdims=True)
    centred = values - average
    spread = jnp.mean(centred * centred, axis=-1, keepdims=True)
    return centred * lax.rsqrt(spread + 1e-05)


def prepare(block, proj_ref):
    normed = normalize(block.astype(F32)).astype(BF16)
    projected = jnp.dot(normed, proj_ref[...], preferred_element_type=F32)
    left = jax.nn.sigmoid(projected[:, 0:128]) * projected[:, 128:256]
    right = jax.nn.sigmoid(projected[:, 256:384]) * projected[:, 384:512]
    return left, right


def output_gate(block, gate_ref):
    normed = normalize(block.astype(F32)).astype(BF16)
    return jax.nn.sigmoid(jnp.dot(normed, gate_ref[...], preferred_element_type=F32))


def finish(block, summed, gate, final_ref):
    mixed = normalize(summed).astype(BF16)
    update = gate * jnp.dot(mixed, final_ref[...], preferred_element_type=F32)
    return (block.astype(F32) + update).astype(BF16)


def outer(a, b):
    a, b = a.astype(F32), b.astype(F32)
    i, j, k = 4, 8, a.shape[0] // 32
    a, b = a.reshape(i, k, 8, 128), b.reshape(j, k, 8, 128)
    total = None
    for n in range(k):
        term = a[:, None, n] * b[None, :, n]
        total = term if total is None else total + term
    return total


def kernel(
    map_in, proj1_in, gate1_in, final1_in, proj2_in, gate2_in, final2_in, out_ref,
    map_ref, proj1, gate1, final1, proj2, gate2, final2, load,
    send_l1, send_r1, left1, right1, send_p1, part1, own1, block1, middle,
    turned, send_l2, send_r2, left2, right2, send_p2, part2, block2,
    out_l1, in_l1, out_a_r1, in_a_r1, out_b_r1, in_b_r1, out_p1, in_p1, out_z, in_z,
    out_a_l2, in_a_l2, out_b_l2, in_b_l2, out_r2, in_r2, out_p2, in_p2, out_t, in_t, far,
):
    row, col = lax.axis_index("row"), lax.axis_index("col")
    y, zl, core = row // 8, row // 2 % 4, row % 2
    x, zh = col // 4, col % 4

    def at(x_, y_, zh_, zl_, core_):
        return (y_ * 8 + zl_ * 2 + core_, x_ * 4 + zh_)

    def plus(value, step):
        return (value + step) % 4

    def minus(value, step):
        return (value + 4 - step) % 4

    flat = x == y
    sibling = at(x, y, zh, zl, 1 - core)
    swapped = at(y, x, zh, zl, core)
    pending, turns = [], []

    def copy(src, dst, send, recv, device):
        return pltpu.make_async_remote_copy(
            src_ref=src, dst_ref=dst, send_sem=send, recv_sem=recv, device_id=device, device_id_type=MESH
        )

    def push(src, dst, send, recv, device):
        c = copy(src, dst, send, recv, device)
        c.start()
        pending.append(c)

    def push_unless(stays, src, dst, send, recv, device):
        c = copy(src, dst, send, recv, device)

        @pl.when(jnp.logical_not(stays))
        def _():
            c.start()

        @pl.when(stays)
        def _():
            pltpu.make_async_copy(src, dst, recv).start()

        turns.append((stays, c))

    def landed(dst, recv):
        copy(dst, dst, out_p2.at[0], recv, sibling).wait_recv()

    loads = [
        pltpu.make_async_copy(src, dst, load.at[n])
        for n, (src, dst) in enumerate((
            (map_in, map_ref), (proj1_in, proj1), (gate1_in, gate1), (final1_in, final1),
            (proj2_in, proj2), (gate2_in, gate2), (final2_in, final2),
        ))
    ]
    for c in loads:
        c.start()

    barrier = pltpu.get_barrier_semaphore()
    greeted = []

    def greet(device, stays=None):
        def signal():
            pl.semaphore_signal(barrier, inc=1, device_id=device, device_id_type=MESH)

        if stays is None:
            signal()
            greeted.append(1)
        else:
            pl.when(jnp.logical_not(stays))(signal)
            greeted.append(1 - stays.astype(jnp.int32))

    for step in (2, 1, 3):
        for side in (0, 1):
            other = (core + side) % 2
            if step != 2:
                greet(at(x, y, plus(zh, step), zl, other))
            greet(at(x, plus(y, step), zh, zl, other))
        greet(at(plus(x, step), y, zh, zl, core))
        greet(at(x, y, zh, plus(zl, step), core))
    greet(sibling)
    greet(swapped, flat)

    for c in loads[:2]:
        c.wait()
    left, right = prepare(map_ref[...].reshape(128, 128), proj1)
    send_r1[...] = right.astype(BF16)
    right1[x, zl] = send_r1[...]
    send_l1[...] = left.astype(BF16)

    pl.semaphore_wait(barrier, sum(greeted))

    for step in (1, 3):
        pl.semaphore_signal(far, inc=1, device_id=at(x, y, plus(zh, step), zl, core), device_id_type=MESH)
    push_unless(flat, send_l1, left1.at[x, core], out_t.at[0], in_t.at[0], swapped)
    for step in (2, 1, 3):
        push(send_r1, right1.at[x, zl], out_a_r1.at[step], in_a_r1.at[zl], at(x, y, zh, plus(zl, step), core))

    def right_over_x(from_zl, n):
        piece = right1.at[x, from_zl]
        return [
            copy(piece, piece, out_b_r1.at[hop, n], in_b_r1.at[x, from_zl], at(plus(x, hop), y, zh, zl, core))
            for hop in (2, 1, 3)
        ]

    for c in right_over_x(zl, 4):
        c.start()
        pending.append(c)
    push_unless(flat, map_ref, block1, out_z.at[0], in_z.at[0], swapped)
    landed(left1.at[y, core], in_t.at[0])
    for step in (2, 1, 3, 0):
        for side in (1, 0):
            if step or side:
                push(left1.at[y, core], left1.at[y, core], out_l1.at[step, side], in_l1.at[y, core],
                     at(x, plus(y, step), zh, zl, (core + side) % 2))
    for step in (2, 1, 3, 0):
        from_zl = plus(zh, step)
        copies = right_over_x(from_zl, step)

        @pl.when(from_zl != zl)
        def _(from_zl=from_zl, copies=copies):
            landed(right1.at[x, from_zl], in_a_r1.at[from_zl])
            for c in copies:
                c.start()

        turns.extend((from_zl == zl, c) for c in copies)

    for step in (0, 1, 3, 2):
        for side in (0, 1):
            if step or side:
                from_, other = minus(y, step), (core + side) % 2
                landed(left1.at[from_, other], in_l1.at[from_, other])
    for step in (2, 1, 3, 0):
        to_zh = plus(zh, step)
        for hop in (1, 3, 2):
            landed(right1.at[minus(x, hop), to_zh], in_b_r1.at[minus(x, hop), to_zh])

        def four_rows(n, _, step=step, to_zh=to_zh):
            half, quarter = n // 2, n % 2
            total = None
            for from_x in range(4):
                term = outer(
                    left1[from_x, half, pl.ds(pl.multiple_of(quarter * 64, 64), 64), :], right1[from_x, to_zh]
                )
                total = term if total is None else total + term
            part = jnp.sum(total, axis=2).reshape(32, 128)
            rows = pl.ds(pl.multiple_of(quarter * 32, 32), 32)
            send_p1[step, half, rows, :] = part.astype(BF16)
            if step == 0:
                own1[half, rows, :] = part
            return 0

        lax.fori_loop(0, 4, four_rows, 0)
        if step == 2:
            pl.semaphore_wait(far, 2)
        for side in (0, 1):
            to = (core + side) % 2
            if step or side:
                push(send_p1.at[step, to], part1.at[step, core], out_p1.at[step, side], in_p1.at[step, core],
                     at(x, y, to_zh, zl, to))

    landed(block1, in_z.at[0])
    for c in loads[2:]:
        c.wait()
    block = block1[...].reshape(128, 128)
    gate = output_gate(block, gate1)
    landed(part1.at[0, 1 - core], in_p1.at[0, 1 - core])
    for step in (1, 3, 2):
        for side in (0, 1):
            landed(part1.at[step, side], in_p1.at[step, side])
    halves = []
    for side in range(2):
        near = jnp.where(core == side, own1[side], part1[0, side].astype(F32))
        rest = part1[1, side].astype(F32) + part1[2, side].astype(F32) + part1[3, side].astype(F32)
        halves.append((near + rest).reshape(8, 1, 8, 128))
    summed = jnp.concatenate(halves, axis=1).reshape(128, 128)
    block = finish(block, summed, gate, final1)
    middle[...] = block.reshape(8, 16, 128)

    left, right = prepare(block, proj2)
    turned[0] = left
    turned[1] = right
    for which, send_ref in ((0, send_l2), (1, send_r2)):
        for j in range(0, 16, 2):
            pair = [turned[which, pl.ds(j + k, 8, stride=16), :] for k in range(2)]
            send_ref[j // 8, (j % 8) * 8 : (j % 8) * 8 + 16, :] = jnp.concatenate(pair, axis=0).astype(BF16)
    left2[x, zh, core] = send_l2[core]
    for step in (2, 1, 3, 0):
        for side in (0, 1):
            to = (core + side) % 2
            if step or side:
                push(send_l2.at[to], left2.at[x, zh, core], out_a_l2.at[step, side], in_a_l2.at[zh, core],
                     at(x, y, plus(zh, step), zl, to))
    push_unless(flat, send_r2, right2.at[x, core], out_t.at[1], in_t.at[1], swapped)
    push_unless(flat, middle, block2, out_z.at[1], in_z.at[1], swapped)

    def left_over_x(step):
        from_zh = minus(zh, step)
        for side in (0, 1):
            if step or side:
                other = (core + side) % 2
                landed(left2.at[x, from_zh, other], in_a_l2.at[from_zh, other])
        piece = left2.at[x, from_zh]
        for hop in (2, 1, 3):
            push(piece, piece, out_b_l2.at[hop, step], in_b_l2.at[x, from_zh], at(plus(x, hop), y, zh, zl, core))

    left_over_x(0)
    landed(right2.at[y, core], in_t.at[1])
    for step in (2, 1, 3, 0):
        for side in (1, 0):
            if step or side:
                push(right2.at[y, core], right2.at[y, core], out_r2.at[step, side], in_r2.at[y, core],
                     at(x, plus(y, step), zh, zl, (core + side) % 2))
    left_over_x(1)
    left_over_x(3)
    landed(block2, in_z.at[1])
    block = block2[...].reshape(128, 128)
    gate = output_gate(block, gate2)
    for step in (0, 1, 3, 2):
        for side in (0, 1):
            if step or side:
                from_, other = minus(y, step), (core + side) % 2
                landed(right2.at[from_, other], in_r2.at[from_, other])
    left_over_x(2)

    for step in (0, 1, 3, 2):
        from_zh = minus(zh, step)
        for hop in (1, 3, 2):
            landed(left2.at[minus(x, hop), from_zh], in_b_l2.at[minus(x, hop), from_zh])

        def four_rows2(quarter, _, step=step, from_zh=from_zh):
            parts = []
            for j_half in range(2):
                total = None
                for from_x in range(4):
                    for other in range(2):
                        term = outer(
                            left2[from_x, from_zh, other, pl.ds(pl.multiple_of(quarter * 32, 32), 32), :],
                            right2[from_x, other, j_half],
                        )
                        total = term if total is None else total + term
                parts.append(jnp.sum(total, axis=2).reshape(4, 1, 8, 128))
            send_p2[step, quarter] = jnp.concatenate(parts, axis=1).reshape(64, 128).astype(BF16)
            return 0

        lax.fori_loop(0, 2, four_rows2, 0)
        push_unless(from_zh == zl, send_p2.at[step], part2.at[zl], out_p2.at[step], in_p2.at[zl],
                    at(x, y, zh, from_zh, core))

    for from_zl in range(4):
        landed(part2.at[from_zl], in_p2.at[from_zl])
    summed = [part2[n].astype(F32).reshape(128, 128) for n in range(4)]
    summed = (summed[0] + summed[1]) + (summed[2] + summed[3])
    out_ref[...] = finish(block, summed, gate, final2).reshape(8, 16, 128)

    for c in pending:
        c.wait_send()
    for stays, c in turns:
        pl.when(jnp.logical_not(stays))(c.wait_send)


def body(*args):
    dma = pltpu.SemaphoreType.DMA
    weights = [pltpu.VMEM((128, 512), BF16), pltpu.VMEM((128, 128), BF16), pltpu.VMEM((128, 128), BF16)]
    tile = pltpu.VMEM((8, 16, 128), BF16)
    return pl.pallas_call(
        kernel,
        out_shape=jax.ShapeDtypeStruct((8, 16, 128), BF16),
        in_specs=[pl.BlockSpec(memory_space=pl.ANY)] * 7,
        out_specs=pl.BlockSpec(memory_space=pltpu.VMEM),
        scratch_shapes=[tile, *weights, *weights, dma((7,))]
        + [pltpu.VMEM((128, 128), BF16)] * 2
        + [pltpu.VMEM((4, 2, 128, 128), BF16), pltpu.VMEM((4, 4, 128, 128), BF16)]
        + [pltpu.VMEM((4, 2, 64, 128), BF16)] * 2
        + [pltpu.VMEM((2, 64, 128), F32), tile, tile]
        + [pltpu.VMEM((2, 128, 128), F32)]
        + [pltpu.VMEM((2, 64, 128), BF16)] * 2
        + [pltpu.VMEM((4, 4, 2, 64, 128), BF16), pltpu.VMEM((4, 2, 2, 64, 128), BF16)]
        + [pltpu.VMEM((4, 2, 64, 128), BF16)] * 2
        + [tile]
        + [dma((4, 2))] * 2 + [dma((4,))] * 2 + [dma((4, 5)), dma((4, 4))] + [dma((4, 2))] * 2 + [dma((2,))] * 2
        + [dma((4, 2))] * 2 + [dma((4, 4))] * 2 + [dma((4, 2))] * 2 + [dma((4,))] * 2 + [dma((2,))] * 2
        + [pltpu.SemaphoreType.REGULAR],
        compiler_params=pltpu.CompilerParams(
            collective_id=0, has_side_effects=True, vmem_limit_bytes=64 * 1024 * 1024 - 65536
        ),
        name="triangles",
    )(*args)


def solution(mesh):
    return jax.shard_map(
        body,
        mesh=mesh,
        in_specs=(P("row", "col", None), P(), P(), P(), P(), P(), P()),
        out_specs=P("row", "col", None),
        check_vma=False,
    )
```

```python
import jax
import jax.numpy as jnp
from jax import lax
from jax.experimental import pallas as pl
from jax.experimental.pallas import tpu as pltpu
from jax.sharding import PartitionSpec as P

MESH = pl.DeviceIdType.MESH
F32 = jnp.float32
BF16 = jnp.bfloat16


def normalize(values):
    average = jnp.mean(values, axis=-1, keepdims=True)
    centred = values - average
    spread = jnp.mean(centred * centred, axis=-1, keepdims=True)
    return centred * lax.rsqrt(spread + 1e-05)


def prepare(block, proj_ref):
    normed = normalize(block.astype(F32)).astype(BF16)
    projected = jnp.dot(normed, proj_ref[...], preferred_element_type=F32)
    left = jax.nn.sigmoid(projected[:, 0:128]) * projected[:, 128:256]
    right = jax.nn.sigmoid(projected[:, 256:384]) * projected[:, 384:512]
    return left, right


def output_gate(block, gate_ref):
    normed = normalize(block.astype(F32)).astype(BF16)
    return jax.nn.sigmoid(jnp.dot(normed, gate_ref[...], preferred_element_type=F32))


def finish(block, summed, gate, final_ref):
    mixed = normalize(summed).astype(BF16)
    update = gate * jnp.dot(mixed, final_ref[...], preferred_element_type=F32)
    return (block.astype(F32) + update).astype(BF16)


def outer(a, b):
    a, b = a.astype(F32), b.astype(F32)
    i, j, k = 4, 8, a.shape[0] // 32
    a, b = a.reshape(i, k, 8, 128), b.reshape(j, k, 8, 128)
    total = None
    for n in range(k):
        term = a[:, None, n] * b[None, :, n]
        total = term if total is None else total + term
    return total


def kernel(
    map_in, proj1_in, gate1_in, final1_in, proj2_in, gate2_in, final2_in, out_ref,
    map_ref, proj1, gate1, final1, proj2, gate2, final2,
    send_l1, send_r1, left1, right1, send_p1, part1, own1, block1, middle,
    turned, send_l2, send_r2, left2, right2, send_p2, part2, block2,
    load, out_turn, out, in_turn, in_z, in_a_r1, in_b_r1, in_l1, in_p1, in_a_l2, in_b_l2, in_r2, in_p2, far,
):
    row, col = lax.axis_index("row"), lax.axis_index("col")
    y, zl, core = row // 8, row // 2 % 4, row % 2
    x, zh = col // 4, col % 4

    def at(x_, y_, zh_, zl_, core_):
        return (y_ * 8 + zl_ * 2 + core_, x_ * 4 + zh_)

    def plus(value, step):
        return (value + step) % 4

    def minus(value, step):
        return (value + 4 - step) % 4

    flat = x == y
    sibling = at(x, y, zh, zl, 1 - core)
    swapped = at(y, x, zh, zl, core)
    zl_sends, y_sends, x_sends, far_sends, near_sends = range(5)

    def copy(src, dst, send, recv, device):
        return pltpu.make_async_remote_copy(
            src_ref=src, dst_ref=dst, send_sem=send, recv_sem=recv, device_id=device, device_id_type=MESH
        )

    def push(src, dst, send, recv, device):
        copy(src, dst, send, recv, device).start()

    def push_unless(stays, src, dst, send, recv, device):
        @pl.when(jnp.logical_not(stays))
        def _():
            copy(src, dst, send, recv, device).start()

        @pl.when(stays)
        def _():
            pltpu.make_async_copy(src, dst, recv).start()

    def landed(like, recv):
        copy(like, like, out_turn.at[0], recv, sibling).wait_recv()

    def sent(like, send):
        copy(like, like, send, in_turn.at[0], sibling).wait_send()

    first_loads = [
        pltpu.make_async_copy(map_in, map_ref, load.at[0]),
        pltpu.make_async_copy(proj1_in, proj1, load.at[1]),
    ]
    later_loads = [
        pltpu.make_async_copy(src, dst, load.at[2])
        for src, dst in (
            (gate1_in, gate1), (final1_in, final1), (proj2_in, proj2), (gate2_in, gate2), (final2_in, final2),
        )
    ]

    barrier = pltpu.get_barrier_semaphore()
    greeted = []

    def greet(device, stays=None):
        def signal():
            pl.semaphore_signal(barrier, inc=1, device_id=device, device_id_type=MESH)

        if stays is None:
            signal()
            greeted.append(1)
        else:
            pl.when(jnp.logical_not(stays))(signal)
            greeted.append(1 - stays.astype(jnp.int32))

    for step in (2, 1, 3):
        for side in (0, 1):
            other = (core + side) % 2
            if step != 2:
                greet(at(x, y, plus(zh, step), zl, other))
            greet(at(x, plus(y, step), zh, zl, other))
        greet(at(plus(x, step), y, zh, zl, core))
        greet(at(x, y, zh, plus(zl, step), core))
    greet(sibling)
    greet(swapped, flat)

    for c in first_loads + later_loads:
        c.start()

    for c in first_loads:
        c.wait()
    left, right = prepare(map_ref[...].reshape(128, 128), proj1)
    send_r1[...] = right.astype(BF16)
    right1[x, zl] = send_r1[...]
    send_l1[...] = left.astype(BF16)

    pl.semaphore_wait(barrier, sum(greeted))

    for step in (1, 3):
        pl.semaphore_signal(far, inc=1, device_id=at(x, y, plus(zh, step), zl, core), device_id_type=MESH)
    push_unless(flat, send_l1, left1.at[2 * x + core], out_turn.at[0], in_turn.at[0], swapped)
    for step in (2, 1, 3):
        push(send_r1, right1.at[x, zl], out.at[0, zl_sends], in_a_r1.at[zl], at(x, y, zh, plus(zl, step), core))

    def right_over_x(from_zl):
        piece = right1.at[x, from_zl]
        for hop in (2, 1, 3):
            push(piece, piece, out.at[0, x_sends], in_b_r1.at[from_zl], at(plus(x, hop), y, zh, zl, core))

    piece = left1.at[2 * y + core]
    landed(piece, in_turn.at[0])
    for step in (2, 1, 3, 0):
        for side in (1, 0):
            if step or side:
                push(piece, piece, out.at[0, y_sends], in_l1, at(x, plus(y, step), zh, zl, (core + side) % 2))
    right_over_x(zl)
    for step in (2, 1, 3, 0):
        from_zl = plus(zh, step)

        @pl.when(from_zl != zl)
        def _(from_zl=from_zl):
            landed(right1.at[x, from_zl], in_a_r1.at[from_zl])
            right_over_x(from_zl)

    push_unless(flat, map_ref, block1, out_turn.at[1], in_z.at[0], swapped)

    landed(left1.at[0:7], in_l1)
    for step in (2, 1, 3, 0):
        to_zh = plus(zh, step)
        landed(right1.at[0, 0:3], in_b_r1.at[to_zh])

        def four_rows(n, _, step=step, to_zh=to_zh):
            half, quarter = n // 2, n % 2
            total = None
            for from_x in range(4):
                term = outer(
                    left1[2 * from_x + half, pl.ds(pl.multiple_of(quarter * 64, 64), 64), :], right1[from_x, to_zh]
                )
                total = term if total is None else total + term
            part = jnp.sum(total, axis=2).reshape(32, 128)
            rows = pl.ds(pl.multiple_of(quarter * 32, 32), 32)
            send_p1[2 * step + half, rows, :] = part.astype(BF16)
            if step == 0:
                own1[half, rows, :] = part
            return 0

        lax.fori_loop(0, 4, four_rows, 0)
        if step == 2:
            pl.semaphore_wait(far, 2)
        for side in (0, 1):
            to = (core + side) % 2
            if step or side:
                push(send_p1.at[2 * step + to], part1.at[2 * step + core], out.at[0, far_sends], in_p1,
                     at(x, y, to_zh, zl, to))

    landed(block1, in_z.at[0])
    pltpu.make_async_copy(left2.at[0:2], left2.at[0:2], load.at[2]).wait()
    block = block1[...].reshape(128, 128)
    gate = output_gate(block, gate1)
    landed(part1.at[0:7], in_p1)
    halves = []
    for side in range(2):
        near = jnp.where(core == side, own1[side], part1[0 + side].astype(F32))
        rest = part1[2 + side].astype(F32) + part1[4 + side].astype(F32) + part1[6 + side].astype(F32)
        halves.append((near + rest).reshape(8, 1, 8, 128))
    summed = jnp.concatenate(halves, axis=1).reshape(128, 128)
    block = finish(block, summed, gate, final1)
    middle[...] = block.reshape(8, 16, 128)

    left, right = prepare(block, proj2)
    turned[0] = left
    turned[1] = right
    for which, send_ref in ((0, send_l2), (1, send_r2)):
        for j in range(0, 16, 2):
            pair = [turned[which, pl.ds(j + k, 8, stride=16), :] for k in range(2)]
            send_ref[j // 8, (j % 8) * 8 : (j % 8) * 8 + 16, :] = jnp.concatenate(pair, axis=0).astype(BF16)
    push_unless(flat, send_r2, right2.at[2 * x + core], out_turn.at[2], in_turn.at[1], swapped)
    left2[x, zh, core] = send_l2[core]
    for step in (0, 1, 3, 2):
        for side in (0, 1):
            to = (core + side) % 2
            if step or side:
                push(send_l2.at[to], left2.at[x, zh, core], out.at[1, far_sends], in_a_l2.at[zh],
                     at(x, y, plus(zh, step), zl, to))
    push_unless(flat, middle, block2, out_turn.at[3], in_z.at[1], swapped)

    def left_over_x(step):
        from_zh = minus(zh, step)
        piece = left2.at[x, from_zh]
        landed(piece if step else left2.at[x, from_zh, 1 - core], in_a_l2.at[from_zh])
        for hop in (2, 1, 3):
            push(piece, piece, out.at[1, x_sends], in_b_l2.at[from_zh], at(plus(x, hop), y, zh, zl, core))

    left_over_x(0)
    piece = right2.at[2 * y + core]
    landed(piece, in_turn.at[1])
    for step in (2, 1, 3, 0):
        for side in (1, 0):
            if step or side:
                push(piece, piece, out.at[1, y_sends], in_r2, at(x, plus(y, step), zh, zl, (core + side) % 2))
    left_over_x(1)
    left_over_x(3)
    left_over_x(2)
    landed(right2.at[0:7], in_r2)

    for step in (0, 1, 3, 2):
        from_zh = minus(zh, step)
        landed(left2.at[0, 0:3], in_b_l2.at[from_zh])

        def four_rows2(quarter, _, step=step, from_zh=from_zh):
            parts = []
            for j_half in range(2):
                total = None
                for from_x in range(4):
                    for other in range(2):
                        term = outer(
                            left2[from_x, from_zh, other, pl.ds(pl.multiple_of(quarter * 32, 32), 32), :],
                            right2[2 * from_x + other, j_half],
                        )
                        total = term if total is None else total + term
                parts.append(jnp.sum(total, axis=2).reshape(4, 1, 8, 128))
            send_p2[step, quarter] = jnp.concatenate(parts, axis=1).reshape(64, 128).astype(BF16)
            return 0

        lax.fori_loop(0, 2, four_rows2, 0)
        push_unless(from_zh == zl, send_p2.at[step], part2.at[zl], out.at[1, near_sends], in_p2,
                    at(x, y, zh, from_zh, core))

    landed(block2, in_z.at[1])
    block = block2[...].reshape(128, 128)
    gate = output_gate(block, gate2)
    landed(part2, in_p2)
    summed = [part2[n].astype(F32).reshape(128, 128) for n in range(4)]
    summed = (summed[0] + summed[1]) + (summed[2] + summed[3])
    out_ref[...] = finish(block, summed, gate, final2).reshape(8, 16, 128)

    sent(right1.at[0, 0:3], out.at[0, zl_sends])
    sent(left1.at[0:7], out.at[0, y_sends])
    sent(right1.at[0:3], out.at[0, x_sends])
    sent(send_p1.at[0:7], out.at[0, far_sends])
    sent(right2.at[0:7], out.at[1, y_sends])
    sent(left2.at[0:3], out.at[1, x_sends])
    sent(part1.at[0:7], out.at[1, far_sends])
    sent(send_p2.at[0:3], out.at[1, near_sends])

    @pl.when(jnp.logical_not(flat))
    def _():
        sent(send_l1, out_turn.at[0])
        sent(block1, out_turn.at[1])
        sent(send_r2, out_turn.at[2])
        sent(block2, out_turn.at[3])


def body(*args):
    dma = pltpu.SemaphoreType.DMA
    weights = [pltpu.VMEM((128, 512), BF16), pltpu.VMEM((128, 128), BF16), pltpu.VMEM((128, 128), BF16)]
    tile = pltpu.VMEM((8, 16, 128), BF16)
    return pl.pallas_call(
        kernel,
        out_shape=jax.ShapeDtypeStruct((8, 16, 128), BF16),
        in_specs=[pl.BlockSpec(memory_space=pl.ANY)] * 7,
        out_specs=pl.BlockSpec(memory_space=pltpu.VMEM),
        scratch_shapes=[tile, *weights, *weights]
        + [pltpu.VMEM((128, 128), BF16)] * 2
        + [pltpu.VMEM((8, 128, 128), BF16), pltpu.VMEM((4, 4, 128, 128), BF16)]
        + [pltpu.VMEM((8, 64, 128), BF16)] * 2
        + [pltpu.VMEM((2, 64, 128), F32), tile, tile]
        + [pltpu.VMEM((2, 128, 128), F32)]
        + [pltpu.VMEM((2, 64, 128), BF16)] * 2
        + [pltpu.VMEM((4, 4, 2, 64, 128), BF16), pltpu.VMEM((8, 2, 64, 128), BF16)]
        + [pltpu.VMEM((4, 2, 64, 128), BF16)] * 2
        + [tile]
        + [dma((3,)), dma((4,)), dma((2, 5)), dma((2,)), dma((2,)), dma((4,)), dma((4,)), dma, dma]
        + [dma((4,)), dma((4,)), dma, dma, pltpu.SemaphoreType.REGULAR],
        compiler_params=pltpu.CompilerParams(
            collective_id=0, has_side_effects=True, vmem_limit_bytes=32 * 1024 * 1024
        ),
        name="triangles",
    )(*[pltpu.with_memory_space_constraint(a, pltpu.HBM) for a in args])


def solution(mesh):
    return jax.shard_map(
        body,
        mesh=mesh,
        in_specs=(P("row", "col", None), P(), P(), P(), P(), P(), P()),
        out_specs=P("row", "col", None),
        check_vma=False,
    )
```

```python
import jax
import jax.numpy as jnp
from jax import lax
from jax.experimental import pallas as pl
from jax.experimental.pallas import tpu as pltpu
from jax.sharding import PartitionSpec as P

MESH = pl.DeviceIdType.MESH
F32 = jnp.float32
BF16 = jnp.bfloat16


def normalize(values):
    average = jnp.mean(values, axis=-1, keepdims=True)
    centred = values - average
    spread = jnp.mean(centred * centred, axis=-1, keepdims=True)
    return centred * lax.rsqrt(spread + 1e-05)


def prepare(block, proj_ref):
    normed = normalize(block.astype(F32)).astype(BF16)
    projected = jnp.dot(normed, proj_ref[...], preferred_element_type=F32)
    left = jax.nn.sigmoid(projected[:, 0:128]) * projected[:, 128:256]
    right = jax.nn.sigmoid(projected[:, 256:384]) * projected[:, 384:512]
    return left, right


def output_gate(block, gate_ref):
    normed = normalize(block.astype(F32)).astype(BF16)
    return jax.nn.sigmoid(jnp.dot(normed, gate_ref[...], preferred_element_type=F32))


def finish(block, summed, gate, final_ref):
    mixed = normalize(summed).astype(BF16)
    update = gate * jnp.dot(mixed, final_ref[...], preferred_element_type=F32)
    return (block.astype(F32) + update).astype(BF16)


def outer(a, b):
    a, b = a.astype(F32), b.astype(F32)
    i, j, k = 4, 8, a.shape[0] // 32
    a, b = a.reshape(i, k, 8, 128), b.reshape(j, k, 8, 128)
    total = None
    for n in range(k):
        term = a[:, None, n] * b[None, :, n]
        total = term if total is None else total + term
    return total


def kernel(
    map_in, proj1_in, gate1_in, final1_in, proj2_in, gate2_in, final2_in, out_ref,
    map_ref, proj1, gate1, final1, proj2, gate2, final2,
    send_l1, send_r1, left1, right1, send_p1, part1, own1, block1, middle,
    turned, send_l2, send_r2, left2, right2, send_p2, part2, block2,
    load, out_turn, out, in_turn, in_z, in_a_r1, in_b_r1, in_l1, in_p1, in_a_l2, in_b_l2, in_r2, in_p2, far,
):
    row, col = lax.axis_index("row"), lax.axis_index("col")
    y, zl, core = row // 8, row // 2 % 4, row % 2
    x, zh = col // 4, col % 4

    def at(x_, y_, zh_, zl_, core_):
        return (y_ * 8 + zl_ * 2 + core_, x_ * 4 + zh_)

    def plus(value, step):
        return (value + step) % 4

    def minus(value, step):
        return (value + 4 - step) % 4

    flat = x == y
    sibling = at(x, y, zh, zl, 1 - core)
    swapped = at(y, x, zh, zl, core)
    zl_sends, y_sends, x_sends, far_sends, near_sends = range(5)

    def copy(src, dst, send, recv, device):
        return pltpu.make_async_remote_copy(
            src_ref=src, dst_ref=dst, send_sem=send, recv_sem=recv, device_id=device, device_id_type=MESH
        )

    def push(src, dst, send, recv, device):
        copy(src, dst, send, recv, device).start()

    def push_unless(stays, src, dst, send, recv, device):
        @pl.when(jnp.logical_not(stays))
        def _():
            copy(src, dst, send, recv, device).start()

        @pl.when(stays)
        def _():
            pltpu.make_async_copy(src, dst, recv).start()

    def landed(like, recv):
        copy(like, like, out_turn.at[0], recv, sibling).wait_recv()

    def sent(like, send):
        copy(like, like, send, in_turn.at[0], sibling).wait_send()

    first_loads = [
        pltpu.make_async_copy(map_in, map_ref, load.at[0]),
        pltpu.make_async_copy(proj1_in, proj1, load.at[1]),
    ]
    later_loads = [
        pltpu.make_async_copy(src, dst, load.at[2])
        for src, dst in (
            (gate1_in, gate1), (final1_in, final1), (proj2_in, proj2), (gate2_in, gate2), (final2_in, final2),
        )
    ]

    barrier = pltpu.get_barrier_semaphore()
    greeted = []

    def greet(device, stays=None):
        def signal():
            pl.semaphore_signal(barrier, inc=1, device_id=device, device_id_type=MESH)

        if stays is None:
            signal()
            greeted.append(1)
        else:
            pl.when(jnp.logical_not(stays))(signal)
            greeted.append(1 - stays.astype(jnp.int32))

    for step in (2, 1, 3):
        for side in (0, 1):
            other = (core + side) % 2
            if step != 2:
                greet(at(x, y, plus(zh, step), zl, other))
            greet(at(x, plus(y, step), zh, zl, other))
        greet(at(plus(x, step), y, zh, zl, core))
        greet(at(x, y, zh, plus(zl, step), core))
    greet(sibling)
    greet(swapped, flat)

    for c in first_loads + later_loads:
        c.start()

    for c in first_loads:
        c.wait()
    left, right = prepare(map_ref[...].reshape(128, 128), proj1)
    send_r1[...] = right.astype(BF16)
    right1[x, zl] = send_r1[...]
    send_l1[...] = left.astype(BF16)

    pl.semaphore_wait(barrier, sum(greeted))

    for step in (1, 3):
        pl.semaphore_signal(far, inc=1, device_id=at(x, y, plus(zh, step), zl, core), device_id_type=MESH)
    push_unless(flat, send_l1, left1.at[2 * x + core], out_turn.at[0], in_turn.at[0], swapped)
    for step in (2, 1, 3):
        push(send_r1, right1.at[x, zl], out.at[0, zl_sends], in_a_r1.at[zl], at(x, y, zh, plus(zl, step), core))

    def right_over_x(from_zl):
        piece = right1.at[x, from_zl]
        for hop in (2, 1, 3):
            push(piece, piece, out.at[0, x_sends], in_b_r1.at[from_zl], at(plus(x, hop), y, zh, zl, core))

    piece = left1.at[2 * y + core]

    def left_over_y(side):
        for step in (2, 1, 3, 0):
            if step or side:
                push(piece, piece, out.at[0, y_sends], in_l1.at[side], at(x, plus(y, step), zh, zl, (core + side) % 2))

    def right_from(step):
        from_zl = plus(zh, step)

        @pl.when(from_zl != zl)
        def _():
            landed(right1.at[x, from_zl], in_a_r1.at[from_zl])
            right_over_x(from_zl)

    right_over_x(zl)
    landed(piece, in_turn.at[0])
    left_over_y(0)
    left_over_y(1)
    right_from(2)
    right_from(1)
    right_from(3)
    right_from(0)
    push_unless(flat, map_ref, block1, out_turn.at[1], in_z.at[0], swapped)

    for side in (0, 1):
        half = (core + side) % 2
        landed(left1.at[0 : 3 + side], in_l1.at[side])
        for step in (2, 1, 3, 0):
            to_zh = plus(zh, step)
            if side == 0:
                landed(right1.at[0, 0:3], in_b_r1.at[to_zh])

            def four_rows(quarter, _, step=step, to_zh=to_zh, half=half):
                total = None
                for from_x in range(4):
                    term = outer(
                        left1[2 * from_x + half, pl.ds(pl.multiple_of(quarter * 64, 64), 64), :], right1[from_x, to_zh]
                    )
                    total = term if total is None else total + term
                part = jnp.sum(total, axis=2).reshape(32, 128)
                rows = pl.ds(pl.multiple_of(quarter * 32, 32), 32)
                send_p1[2 * step + half, rows, :] = part.astype(BF16)
                if step == 0:
                    own1[half, rows, :] = part
                return 0

            lax.fori_loop(0, 2, four_rows, 0)
            if step == 2 and side == 0:
                pl.semaphore_wait(far, 2)
            if step or side:
                push(send_p1.at[2 * step + half], part1.at[2 * step + core], out.at[0, far_sends], in_p1,
                     at(x, y, to_zh, zl, half))

    landed(block1, in_z.at[0])
    pltpu.make_async_copy(left2.at[0:2], left2.at[0:2], load.at[2]).wait()
    block = block1[...].reshape(128, 128)
    gate = output_gate(block, gate1)
    landed(part1.at[0:7], in_p1)
    halves = []
    for side in range(2):
        near = jnp.where(core == side, own1[side], part1[0 + side].astype(F32))
        rest = part1[2 + side].astype(F32) + part1[4 + side].astype(F32) + part1[6 + side].astype(F32)
        halves.append((near + rest).reshape(8, 1, 8, 128))
    summed = jnp.concatenate(halves, axis=1).reshape(128, 128)
    block = finish(block, summed, gate, final1)
    middle[...] = block.reshape(8, 16, 128)

    left, right = prepare(block, proj2)
    turned[0] = left
    turned[1] = right
    for which, send_ref in ((0, send_l2), (1, send_r2)):
        for j in range(0, 16, 2):
            pair = [turned[which, pl.ds(j + k, 8, stride=16), :] for k in range(2)]
            send_ref[j // 8, (j % 8) * 8 : (j % 8) * 8 + 16, :] = jnp.concatenate(pair, axis=0).astype(BF16)
    push_unless(flat, send_r2, right2.at[2 * x + core], out_turn.at[2], in_turn.at[1], swapped)
    left2[x, zh, core] = send_l2[core]
    for step in (0, 1, 3, 2):
        for side in (0, 1):
            to = (core + side) % 2
            if step or side:
                push(send_l2.at[to], left2.at[x, zh, core], out.at[1, far_sends], in_a_l2.at[zh],
                     at(x, y, plus(zh, step), zl, to))
    push_unless(flat, middle, block2, out_turn.at[3], in_z.at[1], swapped)

    def left_over_x(step):
        from_zh = minus(zh, step)
        piece = left2.at[x, from_zh]
        landed(piece if step else left2.at[x, from_zh, 1 - core], in_a_l2.at[from_zh])
        for hop in (2, 1, 3):
            push(piece, piece, out.at[1, x_sends], in_b_l2.at[from_zh], at(plus(x, hop), y, zh, zl, core))

    left_over_x(0)
    piece = right2.at[2 * y + core]
    landed(piece, in_turn.at[1])
    for step in (2, 1, 3, 0):
        for side in (1, 0):
            if step or side:
                push(piece, piece, out.at[1, y_sends], in_r2, at(x, plus(y, step), zh, zl, (core + side) % 2))
    left_over_x(1)
    left_over_x(3)
    left_over_x(2)
    landed(right2.at[0:7], in_r2)

    for step in (0, 1, 3, 2):
        from_zh = minus(zh, step)
        landed(left2.at[0, 0:3], in_b_l2.at[from_zh])

        def four_rows2(quarter, _, step=step, from_zh=from_zh):
            parts = []
            for j_half in range(2):
                total = None
                for from_x in range(4):
                    for other in range(2):
                        term = outer(
                            left2[from_x, from_zh, other, pl.ds(pl.multiple_of(quarter * 32, 32), 32), :],
                            right2[2 * from_x + other, j_half],
                        )
                        total = term if total is None else total + term
                parts.append(jnp.sum(total, axis=2).reshape(4, 1, 8, 128))
            send_p2[step, quarter] = jnp.concatenate(parts, axis=1).reshape(64, 128).astype(BF16)
            return 0

        lax.fori_loop(0, 2, four_rows2, 0)
        push_unless(from_zh == zl, send_p2.at[step], part2.at[zl], out.at[1, near_sends], in_p2,
                    at(x, y, zh, from_zh, core))

    landed(block2, in_z.at[1])
    block = block2[...].reshape(128, 128)
    gate = output_gate(block, gate2)
    landed(part2, in_p2)
    summed = [part2[n].astype(F32).reshape(128, 128) for n in range(4)]
    summed = (summed[0] + summed[1]) + (summed[2] + summed[3])
    out_ref[...] = finish(block, summed, gate, final2).reshape(8, 16, 128)

    sent(right1.at[0, 0:3], out.at[0, zl_sends])
    sent(left1.at[0:7], out.at[0, y_sends])
    sent(right1.at[0:3], out.at[0, x_sends])
    sent(send_p1.at[0:7], out.at[0, far_sends])
    sent(right2.at[0:7], out.at[1, y_sends])
    sent(left2.at[0:3], out.at[1, x_sends])
    sent(part1.at[0:7], out.at[1, far_sends])
    sent(send_p2.at[0:3], out.at[1, near_sends])

    @pl.when(jnp.logical_not(flat))
    def _():
        sent(send_l1, out_turn.at[0])
        sent(block1, out_turn.at[1])
        sent(send_r2, out_turn.at[2])
        sent(block2, out_turn.at[3])


def body(*args):
    dma = pltpu.SemaphoreType.DMA
    weights = [pltpu.VMEM((128, 512), BF16), pltpu.VMEM((128, 128), BF16), pltpu.VMEM((128, 128), BF16)]
    tile = pltpu.VMEM((8, 16, 128), BF16)
    return pl.pallas_call(
        kernel,
        out_shape=jax.ShapeDtypeStruct((8, 16, 128), BF16),
        in_specs=[pl.BlockSpec(memory_space=pl.ANY)] * 7,
        out_specs=pl.BlockSpec(memory_space=pltpu.VMEM),
        scratch_shapes=[tile, *weights, *weights]
        + [pltpu.VMEM((128, 128), BF16)] * 2
        + [pltpu.VMEM((8, 128, 128), BF16), pltpu.VMEM((4, 4, 128, 128), BF16)]
        + [pltpu.VMEM((8, 64, 128), BF16)] * 2
        + [pltpu.VMEM((2, 64, 128), F32), tile, tile]
        + [pltpu.VMEM((2, 128, 128), F32)]
        + [pltpu.VMEM((2, 64, 128), BF16)] * 2
        + [pltpu.VMEM((4, 4, 2, 64, 128), BF16), pltpu.VMEM((8, 2, 64, 128), BF16)]
        + [pltpu.VMEM((4, 2, 64, 128), BF16)] * 2
        + [tile]
        + [dma((3,)), dma((4,)), dma((2, 5)), dma((2,)), dma((2,)), dma((4,)), dma((4,)), dma((2,)), dma]
        + [dma((4,)), dma((4,)), dma, dma, pltpu.SemaphoreType.REGULAR],
        compiler_params=pltpu.CompilerParams(
            collective_id=0, has_side_effects=True, vmem_limit_bytes=32 * 1024 * 1024
        ),
        name="triangles",
    )(*[pltpu.with_memory_space_constraint(a, pltpu.HBM) for a in args])


def solution(mesh):
    return jax.shard_map(
        body,
        mesh=mesh,
        in_specs=(P("row", "col", None), P(), P(), P(), P(), P(), P()),
        out_specs=P("row", "col", None),
        check_vma=False,
    )
```

```python
import jax
import jax.numpy as jnp
from jax import lax
from jax.experimental import pallas as pl
from jax.experimental.pallas import tpu as pltpu
from jax.sharding import PartitionSpec as P

MESH = pl.DeviceIdType.MESH
F32 = jnp.float32
BF16 = jnp.bfloat16


def normalize(values):
    average = jnp.mean(values, axis=-1, keepdims=True)
    centred = values - average
    spread = jnp.mean(centred * centred, axis=-1, keepdims=True)
    return centred * lax.rsqrt(spread + 1e-05)


def prepare(block, proj_ref):
    normed = normalize(block.astype(F32)).astype(BF16)
    projected = jnp.dot(normed, proj_ref[...], preferred_element_type=F32)
    left = jax.nn.sigmoid(projected[:, 0:128]) * projected[:, 128:256]
    right = jax.nn.sigmoid(projected[:, 256:384]) * projected[:, 384:512]
    return left, right


def output_gate(block, gate_ref):
    normed = normalize(block.astype(F32)).astype(BF16)
    return jax.nn.sigmoid(jnp.dot(normed, gate_ref[...], preferred_element_type=F32))


def finish(block, summed, gate, final_ref):
    mixed = normalize(summed).astype(BF16)
    update = gate * jnp.dot(mixed, final_ref[...], preferred_element_type=F32)
    return (block.astype(F32) + update).astype(BF16)


def outer(a, b):
    a, b = a.astype(F32), b.astype(F32)
    i, j, k = 4, 8, a.shape[0] // 32
    a, b = a.reshape(i, k, 8, 128), b.reshape(j, k, 8, 128)
    total = None
    for n in range(k):
        term = a[:, None, n] * b[None, :, n]
        total = term if total is None else total + term
    return total


def kernel(
    map_in, proj1_in, gate1_in, final1_in, proj2_in, gate2_in, final2_in, out_ref,
    map_ref, proj1, gate1, final1, proj2, gate2, final2,
    send_z, send_l1, send_r1, left1, right1, send_p1, part1, own1, block1, middle,
    turned, send_l2, send_r2, left2, right2, send_p2, part2, block2,
    load, out_turn, out, in_turn, in_z, in_a_r1, in_b_r1, in_l1, in_p1, in_a_l2, in_b_l2, in_r2, in_p2, far,
):
    row, col = lax.axis_index("row"), lax.axis_index("col")
    y, zl, core = row // 8, row // 2 % 4, row % 2
    x, zh = col // 4, col % 4

    def at(x_, y_, zh_, zl_, core_):
        return (y_ * 8 + zl_ * 2 + core_, x_ * 4 + zh_)

    def plus(value, step):
        return (value + step) % 4

    def minus(value, step):
        return (value + 4 - step) % 4

    flat = x == y
    sibling = at(x, y, zh, zl, 1 - core)
    swapped = at(y, x, zh, zl, core)
    zl_sends, y_sends, x_sends, far_sends, near_sends = range(5)

    def copy(src, dst, send, recv, device):
        return pltpu.make_async_remote_copy(
            src_ref=src, dst_ref=dst, send_sem=send, recv_sem=recv, device_id=device, device_id_type=MESH
        )

    def push(src, dst, send, recv, device):
        copy(src, dst, send, recv, device).start()

    def push_unless(stays, src, dst, send, recv, device):
        @pl.when(jnp.logical_not(stays))
        def _():
            copy(src, dst, send, recv, device).start()

        @pl.when(stays)
        def _():
            pltpu.make_async_copy(src, dst, recv).start()

    def landed(like, recv):
        copy(like, like, out_turn.at[0], recv, sibling).wait_recv()

    def sent(like, send):
        copy(like, like, send, in_turn.at[0], sibling).wait_send()

    first_loads = [
        pltpu.make_async_copy(map_in, map_ref, load.at[0]),
        pltpu.make_async_copy(proj1_in, proj1, load.at[1]),
    ]
    later_loads = [
        pltpu.make_async_copy(src, dst, load.at[2])
        for src, dst in (
            (gate1_in, gate1), (final1_in, final1), (proj2_in, proj2), (gate2_in, gate2), (final2_in, final2),
        )
    ]

    barrier = pltpu.get_barrier_semaphore()
    greeted = []

    def greet(device, stays=None):
        def signal():
            pl.semaphore_signal(barrier, inc=1, device_id=device, device_id_type=MESH)

        if stays is None:
            signal()
            greeted.append(1)
        else:
            pl.when(jnp.logical_not(stays))(signal)
            greeted.append(1 - stays.astype(jnp.int32))

    for step in (2, 1, 3):
        if step != 2:
            greet(at(x, y, plus(zh, step), zl, core))
        for side in (0, 1):
            greet(at(x, plus(y, step), zh, zl, (core + side) % 2))
        greet(at(plus(x, step), y, zh, zl, core))
        greet(at(x, y, zh, plus(zl, step), core))
    greet(sibling)
    greet(swapped, flat)
    greet(at(y, x, zh, zl, 1 - core))

    for c in first_loads + later_loads:
        c.start()

    for c in first_loads:
        c.wait()
    left, right = prepare(map_ref[...].reshape(128, 128), proj1)
    columns = map_ref[...].astype(F32).reshape(8, 2, 8, 128)
    for side in range(2):
        send_z[side] = columns[:, side].reshape(64, 128).astype(BF16)
    send_r1[...] = right.astype(BF16)
    right1[x, zl] = send_r1[...]
    send_l1[...] = left.astype(BF16)

    pl.semaphore_wait(barrier, sum(greeted))

    for step in (1, 3):
        pl.semaphore_signal(far, inc=1, device_id=at(x, y, plus(zh, step), zl, core), device_id_type=MESH)
    push_unless(flat, send_l1, left1.at[2 * x + core], out_turn.at[0], in_turn.at[0], swapped)
    for step in (2, 1, 3):
        push(send_r1, right1.at[x, zl], out.at[0, zl_sends], in_a_r1.at[zl], at(x, y, zh, plus(zl, step), core))

    def right_over_x(from_zl):
        piece = right1.at[x, from_zl]
        for hop in (2, 1, 3):
            push(piece, piece, out.at[0, x_sends], in_b_r1.at[from_zl], at(plus(x, hop), y, zh, zl, core))

    piece = left1.at[2 * y + core]

    def left_over_y(side):
        for step in (2, 1, 3, 0):
            if step or side:
                push(piece, piece, out.at[0, y_sends], in_l1.at[side], at(x, plus(y, step), zh, zl, (core + side) % 2))

    def right_from(step):
        from_zl = plus(zh, step)

        @pl.when(from_zl != zl)
        def _():
            landed(right1.at[x, from_zl], in_a_r1.at[from_zl])
            right_over_x(from_zl)

    right_over_x(zl)
    landed(piece, in_turn.at[0])
    left_over_y(0)
    left_over_y(1)
    right_from(2)
    right_from(1)
    right_from(3)
    right_from(0)
    push_unless(flat, send_z.at[core], block1.at[core], out_turn.at[1], in_z.at[0], swapped)
    push(send_z.at[1 - core], block1.at[core], out.at[0, near_sends], in_z.at[0], at(y, x, zh, zl, 1 - core))

    for side in (0, 1):
        half = (core + side) % 2
        landed(left1.at[0 : 3 + side], in_l1.at[side])
        for step in (2, 1, 3, 0):
            to_zh = plus(zh, step)
            if side == 0:
                landed(right1.at[0, 0:3], in_b_r1.at[to_zh])

            def four_rows(quarter, _, step=step, to_zh=to_zh, half=half):
                total = None
                for from_x in range(4):
                    term = outer(
                        left1[2 * from_x + half, pl.ds(pl.multiple_of(quarter * 64, 64), 64), :], right1[from_x, to_zh]
                    )
                    total = term if total is None else total + term
                part = jnp.sum(total, axis=2).reshape(32, 128)
                rows = pl.ds(pl.multiple_of(quarter * 32, 32), 32)
                send_p1[2 * step + half, rows, :] = part.astype(BF16)
                if step == 0:
                    own1[half, rows, :] = part
                return 0

            lax.fori_loop(0, 2, four_rows, 0)
            if step == 2 and side == 0:
                pl.semaphore_wait(far, 2)
            if step:
                push(send_p1.at[2 * step + half], part1.at[2 * step + half], out.at[0, far_sends], in_p1,
                     at(x, y, to_zh, zl, core))

    landed(block1, in_z.at[0])
    pltpu.make_async_copy(left2.at[0:2], left2.at[0:2], load.at[2]).wait()
    block = block1[...].reshape(128, 128)
    gate = output_gate(block, gate1)
    landed(part1.at[0:6], in_p1)
    halves = [
        (own1[n] + part1[2 + n].astype(F32)) + (part1[4 + n].astype(F32) + part1[6 + n].astype(F32)) for n in range(2)
    ]
    summed = jnp.concatenate(halves, axis=0)
    block = finish(block, summed, gate, final1)
    middle[...] = block.reshape(2, 64, 128)

    left, right = prepare(block, proj2)
    turned[0] = left
    turned[1] = right
    for which, send_ref in ((0, send_l2), (1, send_r2)):
        for half in range(2):
            for j in range(0, 8, 2):
                pair = [turned[which, pl.ds(64 * half + j + k, 8, stride=8), :] for k in range(2)]
                send_ref[half, j * 8 : j * 8 + 16, :] = jnp.concatenate(pair, axis=0).astype(BF16)
    push_unless(flat, send_r2, right2.at[2 * x + core], out_turn.at[2], in_turn.at[1], swapped)
    left2[x, zh] = send_l2[...]
    for step in (1, 3, 2):
        push(send_l2, left2.at[x, zh], out.at[1, far_sends], in_a_l2.at[zh], at(x, y, plus(zh, step), zl, core))
    push_unless(flat, middle.at[core], block2.at[core], out_turn.at[3], in_z.at[1], swapped)
    push(middle.at[1 - core], block2.at[core], out.at[1, zl_sends], in_z.at[1], at(y, x, zh, zl, 1 - core))

    def left_over_x(step):
        from_zh = minus(zh, step)
        piece = left2.at[x, from_zh]
        if step:
            landed(piece, in_a_l2.at[from_zh])
        for hop in (2, 1, 3):
            push(piece, piece, out.at[1, x_sends], in_b_l2.at[from_zh], at(plus(x, hop), y, zh, zl, core))

    left_over_x(0)
    piece = right2.at[2 * y + core]
    landed(piece, in_turn.at[1])
    for step in (2, 1, 3, 0):
        for side in (1, 0):
            if step or side:
                push(piece, piece, out.at[1, y_sends], in_r2, at(x, plus(y, step), zh, zl, (core + side) % 2))
    left_over_x(1)
    left_over_x(3)
    left_over_x(2)
    landed(right2.at[0:7], in_r2)

    for step in (0, 1, 3, 2):
        from_zh = minus(zh, step)
        landed(left2.at[0, 0:3], in_b_l2.at[from_zh])

        def four_rows2(quarter, _, step=step, from_zh=from_zh):
            parts = []
            for j_half in range(2):
                total = None
                for from_x in range(4):
                    for other in range(2):
                        term = outer(
                            left2[from_x, from_zh, other, pl.ds(pl.multiple_of(quarter * 32, 32), 32), :],
                            right2[2 * from_x + j_half, other],
                        )
                        total = term if total is None else total + term
                parts.append(jnp.sum(total, axis=2).reshape(4, 1, 8, 128))
            send_p2[step, quarter] = jnp.concatenate(parts, axis=1).reshape(64, 128).astype(BF16)
            return 0

        for quarter in range(2):
            four_rows2(quarter, 0)
            push_unless(from_zh == zl, send_p2.at[step, quarter], part2.at[zl, quarter], out.at[1, near_sends], in_p2,
                        at(x, y, zh, from_zh, core))

    landed(block2, in_z.at[1])
    block = jnp.concatenate([block2[n].astype(F32).reshape(8, 1, 8, 128) for n in range(2)], axis=1).reshape(128, 128)
    gate = output_gate(block, gate2)
    landed(part2, in_p2)
    summed = [part2[n].astype(F32).reshape(128, 128) for n in range(4)]
    summed = (summed[0] + summed[1]) + (summed[2] + summed[3])
    out_ref[...] = finish(block, summed, gate, final2).reshape(8, 16, 128)

    sent(right1.at[0, 0:3], out.at[0, zl_sends])
    sent(left1.at[0:7], out.at[0, y_sends])
    sent(right1.at[0:3], out.at[0, x_sends])
    sent(send_p1.at[0:6], out.at[0, far_sends])
    sent(send_z.at[0], out.at[0, near_sends])
    sent(right2.at[0:7], out.at[1, y_sends])
    sent(left2.at[0:3], out.at[1, x_sends])
    sent(left2.at[0, 0:3], out.at[1, far_sends])
    sent(middle.at[0], out.at[1, zl_sends])
    sent(send_p2.at[0:3], out.at[1, near_sends])

    @pl.when(jnp.logical_not(flat))
    def _():
        sent(send_l1, out_turn.at[0])
        sent(block1.at[0], out_turn.at[1])
        sent(send_r2, out_turn.at[2])
        sent(block2.at[0], out_turn.at[3])


def body(*args):
    dma = pltpu.SemaphoreType.DMA
    weights = [pltpu.VMEM((128, 512), BF16), pltpu.VMEM((128, 128), BF16), pltpu.VMEM((128, 128), BF16)]
    tile = pltpu.VMEM((8, 16, 128), BF16)
    return pl.pallas_call(
        kernel,
        out_shape=jax.ShapeDtypeStruct((8, 16, 128), BF16),
        in_specs=[pl.BlockSpec(memory_space=pl.ANY)] * 7,
        out_specs=pl.BlockSpec(memory_space=pltpu.VMEM),
        scratch_shapes=[tile, *weights, *weights]
        + [pltpu.VMEM((2, 64, 128), BF16)]
        + [pltpu.VMEM((128, 128), BF16)] * 2
        + [pltpu.VMEM((8, 128, 128), BF16), pltpu.VMEM((4, 4, 128, 128), BF16)]
        + [pltpu.VMEM((8, 64, 128), BF16)] * 2
        + [pltpu.VMEM((2, 64, 128), F32)] + [pltpu.VMEM((2, 64, 128), BF16)] * 2
        + [pltpu.VMEM((2, 128, 128), F32)]
        + [pltpu.VMEM((2, 64, 128), BF16)] * 2
        + [pltpu.VMEM((4, 4, 2, 64, 128), BF16), pltpu.VMEM((8, 2, 64, 128), BF16)]
        + [pltpu.VMEM((4, 2, 64, 128), BF16)] * 2
        + [pltpu.VMEM((2, 64, 128), BF16)]
        + [dma((3,)), dma((4,)), dma((2, 5)), dma((2,)), dma((2,)), dma((4,)), dma((4,)), dma((2,)), dma]
        + [dma((4,)), dma((4,)), dma, dma, pltpu.SemaphoreType.REGULAR],
        compiler_params=pltpu.CompilerParams(
            collective_id=0, has_side_effects=True, vmem_limit_bytes=32 * 1024 * 1024
        ),
        name="triangles",
    )(*[pltpu.with_memory_space_constraint(a, pltpu.HBM) for a in args])


def solution(mesh):
    return jax.shard_map(
        body,
        mesh=mesh,
        in_specs=(P("row", "col", None), P(), P(), P(), P(), P(), P()),
        out_specs=P("row", "col", None),
        check_vma=False,
    )
```

```python
import jax
import jax.numpy as jnp
from jax import lax
from jax.experimental import pallas as pl
from jax.experimental.pallas import tpu as pltpu
from jax.sharding import PartitionSpec as P

MESH = pl.DeviceIdType.MESH
F32 = jnp.float32
BF16 = jnp.bfloat16


def normalize(values):
    average = jnp.mean(values, axis=-1, keepdims=True)
    centred = values - average
    spread = jnp.mean(centred * centred, axis=-1, keepdims=True)
    return centred * lax.rsqrt(spread + 1e-05)


def prepare(block, proj_ref):
    normed = normalize(block.astype(F32)).astype(BF16)
    projected = jnp.dot(normed, proj_ref[...], preferred_element_type=F32)
    left = jax.nn.sigmoid(projected[:, 0:128]) * projected[:, 128:256]
    right = jax.nn.sigmoid(projected[:, 256:384]) * projected[:, 384:512]
    return left, right


def output_gate(block, gate_ref):
    normed = normalize(block.astype(F32)).astype(BF16)
    return jax.nn.sigmoid(jnp.dot(normed, gate_ref[...], preferred_element_type=F32))


def finish(block, summed, gate, final_ref):
    mixed = normalize(summed).astype(BF16)
    update = gate * jnp.dot(mixed, final_ref[...], preferred_element_type=F32)
    return (block.astype(F32) + update).astype(BF16)


def outer(a, b):
    a, b = a.astype(F32), b.astype(F32)
    i, j, k = 4, 8, a.shape[0] // 32
    a, b = a.reshape(i, k, 8, 128), b.reshape(j, k, 8, 128)
    total = None
    for n in range(k):
        term = a[:, None, n] * b[None, :, n]
        total = term if total is None else total + term
    return total


def kernel(
    map_in, proj1_in, gate1_in, final1_in, proj2_in, gate2_in, final2_in, out_ref,
    map_ref, proj1, gate1, final1, proj2, gate2, final2,
    send_z, send_l1, send_r1, left1, right1, send_p1, part1, own1, block1, middle,
    turned, send_l2, send_r2, left2, right2, send_p2, part2, block2,
    load, out_turn, out, in_turn, in_z, in_a_r1, in_b_r1, in_l1, in_p1, in_a_l2, in_b_l2, in_r2, in_p2, far,
):
    row, col = lax.axis_index("row"), lax.axis_index("col")
    y, zl, core = row // 8, row // 2 % 4, row % 2
    x, zh = col // 4, col % 4

    def at(x_, y_, zh_, zl_, core_):
        return (y_ * 8 + zl_ * 2 + core_, x_ * 4 + zh_)

    def plus(value, step):
        return (value + step) % 4

    def minus(value, step):
        return (value + 4 - step) % 4

    flat = x == y
    sibling = at(x, y, zh, zl, 1 - core)
    swapped = at(y, x, zh, zl, core)
    zl_sends, y_sends, x_sends, far_sends, near_sends = range(5)

    def copy(src, dst, send, recv, device):
        return pltpu.make_async_remote_copy(
            src_ref=src, dst_ref=dst, send_sem=send, recv_sem=recv, device_id=device, device_id_type=MESH
        )

    def push(src, dst, send, recv, device):
        copy(src, dst, send, recv, device).start()

    def push_unless(stays, src, dst, send, recv, device):
        @pl.when(jnp.logical_not(stays))
        def _():
            copy(src, dst, send, recv, device).start()

        @pl.when(stays)
        def _():
            pltpu.make_async_copy(src, dst, recv).start()

    def landed(like, recv):
        copy(like, like, out_turn.at[0], recv, sibling).wait_recv()

    def sent(like, send):
        copy(like, like, send, in_turn.at[0], sibling).wait_send()

    first_loads = [
        pltpu.make_async_copy(map_in, map_ref, load.at[0]),
        pltpu.make_async_copy(proj1_in, proj1, load.at[1]),
    ]
    later_loads = [
        pltpu.make_async_copy(src, dst, load.at[2])
        for src, dst in (
            (gate1_in, gate1), (final1_in, final1), (proj2_in, proj2), (gate2_in, gate2), (final2_in, final2),
        )
    ]

    barrier = pltpu.get_barrier_semaphore()
    greeted = []

    def greet(device, stays=None):
        def signal():
            pl.semaphore_signal(barrier, inc=1, device_id=device, device_id_type=MESH)

        if stays is None:
            signal()
            greeted.append(1)
        else:
            pl.when(jnp.logical_not(stays))(signal)
            greeted.append(1 - stays.astype(jnp.int32))

    for step in (2, 1, 3):
        if step != 2:
            greet(at(x, y, plus(zh, step), zl, core))
        for side in (0, 1):
            greet(at(x, plus(y, step), zh, zl, (core + side) % 2))
        greet(at(plus(x, step), y, zh, zl, core))
        greet(at(x, y, zh, plus(zl, step), core))
    greet(sibling)
    greet(swapped, flat)
    greet(at(y, x, zh, zl, 1 - core))

    for c in first_loads + later_loads:
        c.start()

    for c in first_loads:
        c.wait()
    left, right = prepare(map_ref[...].reshape(128, 128), proj1)
    columns = map_ref[...].astype(F32).reshape(8, 2, 8, 128)
    for side in range(2):
        send_z[side] = columns[:, side].reshape(64, 128).astype(BF16)
    send_r1[...] = right.astype(BF16)
    right1[x, zl] = send_r1[...]
    send_l1[...] = left.astype(BF16)

    pl.semaphore_wait(barrier, sum(greeted))

    for step in (1, 3):
        pl.semaphore_signal(far, inc=1, device_id=at(x, y, plus(zh, step), zl, core), device_id_type=MESH)
    push_unless(flat, send_l1, left1.at[2 * x + core], out_turn.at[0], in_turn.at[0], swapped)
    for step in (2, 1, 3):
        push(send_r1, right1.at[x, zl], out.at[0, zl_sends], in_a_r1.at[zl], at(x, y, zh, plus(zl, step), core))

    def right_over_x(from_zl):
        piece = right1.at[x, from_zl]
        for hop in (1, 3, 2):
            push(piece, piece, out.at[0, x_sends], in_b_r1.at[from_zl], at(plus(x, hop), y, zh, zl, core))

    piece = left1.at[2 * y + core]

    def left_over_y(side):
        for step in (1, 3, 2, 0):
            if step or side:
                push(piece, piece, out.at[0, y_sends], in_l1.at[side], at(x, plus(y, step), zh, zl, (core + side) % 2))

    def right_from(step):
        from_zl = plus(zh, step)

        @pl.when(from_zl != zl)
        def _():
            landed(right1.at[x, from_zl], in_a_r1.at[from_zl])
            right_over_x(from_zl)

    right_over_x(zl)
    landed(piece, in_turn.at[0])
    left_over_y(0)
    left_over_y(1)
    right_from(2)
    right_from(1)
    right_from(3)
    right_from(0)
    push_unless(flat, send_z.at[core], block1.at[core], out_turn.at[1], in_z.at[0], swapped)
    push(send_z.at[1 - core], block1.at[core], out.at[0, near_sends], in_z.at[0], at(y, x, zh, zl, 1 - core))

    for side in (0, 1):
        half = (core + side) % 2
        landed(left1.at[0 : 3 + side], in_l1.at[side])
        for step in (2, 1, 3, 0):
            to_zh = plus(zh, step)
            if side == 0:
                landed(right1.at[0, 0:3], in_b_r1.at[to_zh])

            def four_rows(quarter, _, step=step, to_zh=to_zh, half=half):
                total = None
                for from_x in range(4):
                    term = outer(
                        left1[2 * from_x + half, pl.ds(pl.multiple_of(quarter * 64, 64), 64), :], right1[from_x, to_zh]
                    )
                    total = term if total is None else total + term
                part = jnp.sum(total, axis=2).reshape(32, 128)
                rows = pl.ds(pl.multiple_of(quarter * 32, 32), 32)
                send_p1[2 * step + half, rows, :] = part.astype(BF16)
                if step == 0:
                    own1[half, rows, :] = part
                return 0

            lax.fori_loop(0, 2, four_rows, 0)
            if step == 2 and side == 0:
                pl.semaphore_wait(far, 2)
            if step:
                push(send_p1.at[2 * step + half], part1.at[2 * step + half], out.at[0, far_sends], in_p1,
                     at(x, y, to_zh, zl, core))

    landed(block1, in_z.at[0])
    pltpu.make_async_copy(left2.at[0:2], left2.at[0:2], load.at[2]).wait()
    block = block1[...].reshape(128, 128)
    gate = output_gate(block, gate1)
    landed(part1.at[0:6], in_p1)
    halves = [
        (own1[n] + part1[2 + n].astype(F32)) + (part1[4 + n].astype(F32) + part1[6 + n].astype(F32)) for n in range(2)
    ]
    summed = jnp.concatenate(halves, axis=0)
    block = finish(block, summed, gate, final1)
    middle[...] = block.reshape(2, 64, 128)

    left, right = prepare(block, proj2)
    turned[0] = left
    turned[1] = right
    for which, send_ref in ((0, send_l2), (1, send_r2)):
        for half in range(2):
            for j in range(0, 8, 2):
                pair = [turned[which, pl.ds(64 * half + j + k, 8, stride=8), :] for k in range(2)]
                send_ref[half, j * 8 : j * 8 + 16, :] = jnp.concatenate(pair, axis=0).astype(BF16)
    push_unless(flat, send_r2, right2.at[2 * x + core], out_turn.at[2], in_turn.at[1], swapped)
    left2[x, zh] = send_l2[...]
    for step in (1, 3, 2):
        push(send_l2, left2.at[x, zh], out.at[1, far_sends], in_a_l2.at[zh], at(x, y, plus(zh, step), zl, core))
    push_unless(flat, middle.at[core], block2.at[core], out_turn.at[3], in_z.at[1], swapped)
    push(middle.at[1 - core], block2.at[core], out.at[1, zl_sends], in_z.at[1], at(y, x, zh, zl, 1 - core))

    def left_over_x(step):
        from_zh = minus(zh, step)
        piece = left2.at[x, from_zh]
        if step:
            landed(piece, in_a_l2.at[from_zh])
        for hop in (1, 3, 2):
            push(piece, piece, out.at[1, x_sends], in_b_l2.at[from_zh], at(plus(x, hop), y, zh, zl, core))

    left_over_x(0)
    piece = right2.at[2 * y + core]
    landed(piece, in_turn.at[1])
    for step in (2, 1, 3, 0):
        for side in (1, 0):
            if step or side:
                push(piece, piece, out.at[1, y_sends], in_r2, at(x, plus(y, step), zh, zl, (core + side) % 2))
    left_over_x(1)
    left_over_x(3)
    left_over_x(2)
    landed(right2.at[0:7], in_r2)

    for step in (0, 1, 3, 2):
        from_zh = minus(zh, step)
        landed(left2.at[0, 0:3], in_b_l2.at[from_zh])

        def four_rows2(quarter, _, step=step, from_zh=from_zh):
            parts = []
            for j_half in range(2):
                total = None
                for from_x in range(4):
                    for other in range(2):
                        term = outer(
                            left2[from_x, from_zh, other, pl.ds(pl.multiple_of(quarter * 32, 32), 32), :],
                            right2[2 * from_x + j_half, other],
                        )
                        total = term if total is None else total + term
                parts.append(jnp.sum(total, axis=2).reshape(4, 1, 8, 128))
            send_p2[step, quarter] = jnp.concatenate(parts, axis=1).reshape(64, 128).astype(BF16)
            return 0

        for quarter in range(2):
            four_rows2(quarter, 0)
            push_unless(from_zh == zl, send_p2.at[step, quarter], part2.at[zl, quarter], out.at[1, near_sends], in_p2,
                        at(x, y, zh, from_zh, core))

    landed(block2, in_z.at[1])
    block = jnp.concatenate([block2[n].astype(F32).reshape(8, 1, 8, 128) for n in range(2)], axis=1).reshape(128, 128)
    gate = output_gate(block, gate2)
    landed(part2, in_p2)
    summed = [part2[n].astype(F32).reshape(128, 128) for n in range(4)]
    summed = (summed[0] + summed[1]) + (summed[2] + summed[3])
    out_ref[...] = finish(block, summed, gate, final2).reshape(8, 16, 128)

    sent(right1.at[0, 0:3], out.at[0, zl_sends])
    sent(left1.at[0:7], out.at[0, y_sends])
    sent(right1.at[0:3], out.at[0, x_sends])
    sent(send_p1.at[0:6], out.at[0, far_sends])
    sent(send_z.at[0], out.at[0, near_sends])
    sent(right2.at[0:7], out.at[1, y_sends])
    sent(left2.at[0:3], out.at[1, x_sends])
    sent(left2.at[0, 0:3], out.at[1, far_sends])
    sent(middle.at[0], out.at[1, zl_sends])
    sent(send_p2.at[0:3], out.at[1, near_sends])

    @pl.when(jnp.logical_not(flat))
    def _():
        sent(send_l1, out_turn.at[0])
        sent(block1.at[0], out_turn.at[1])
        sent(send_r2, out_turn.at[2])
        sent(block2.at[0], out_turn.at[3])


def body(*args):
    dma = pltpu.SemaphoreType.DMA
    weights = [pltpu.VMEM((128, 512), BF16), pltpu.VMEM((128, 128), BF16), pltpu.VMEM((128, 128), BF16)]
    tile = pltpu.VMEM((8, 16, 128), BF16)
    return pl.pallas_call(
        kernel,
        out_shape=jax.ShapeDtypeStruct((8, 16, 128), BF16),
        in_specs=[pl.BlockSpec(memory_space=pl.ANY)] * 7,
        out_specs=pl.BlockSpec(memory_space=pltpu.VMEM),
        scratch_shapes=[tile, *weights, *weights]
        + [pltpu.VMEM((2, 64, 128), BF16)]
        + [pltpu.VMEM((128, 128), BF16)] * 2
        + [pltpu.VMEM((8, 128, 128), BF16), pltpu.VMEM((4, 4, 128, 128), BF16)]
        + [pltpu.VMEM((8, 64, 128), BF16)] * 2
        + [pltpu.VMEM((2, 64, 128), F32)] + [pltpu.VMEM((2, 64, 128), BF16)] * 2
        + [pltpu.VMEM((2, 128, 128), F32)]
        + [pltpu.VMEM((2, 64, 128), BF16)] * 2
        + [pltpu.VMEM((4, 4, 2, 64, 128), BF16), pltpu.VMEM((8, 2, 64, 128), BF16)]
        + [pltpu.VMEM((4, 2, 64, 128), BF16)] * 2
        + [pltpu.VMEM((2, 64, 128), BF16)]
        + [dma((3,)), dma((4,)), dma((2, 5)), dma((2,)), dma((2,)), dma((4,)), dma((4,)), dma((2,)), dma]
        + [dma((4,)), dma((4,)), dma, dma, pltpu.SemaphoreType.REGULAR],
        compiler_params=pltpu.CompilerParams(
            collective_id=0, has_side_effects=True, vmem_limit_bytes=32 * 1024 * 1024
        ),
        name="triangles",
    )(*[pltpu.with_memory_space_constraint(a, pltpu.HBM) for a in args])


def solution(mesh):
    return jax.shard_map(
        body,
        mesh=mesh,
        in_specs=(P("row", "col", None), P(), P(), P(), P(), P(), P()),
        out_specs=P("row", "col", None),
        check_vma=False,
    )
```

```python
import jax
import jax.numpy as jnp
from jax import lax
from jax.experimental import pallas as pl
from jax.experimental.pallas import tpu as pltpu
from jax.sharding import PartitionSpec as P

MESH = pl.DeviceIdType.MESH
F32 = jnp.float32
BF16 = jnp.bfloat16


def normalize(values):
    average = jnp.mean(values, axis=-1, keepdims=True)
    centred = values - average
    spread = jnp.mean(centred * centred, axis=-1, keepdims=True)
    return centred * lax.rsqrt(spread + 1e-05)


def prepare(block, proj_ref):
    normed = normalize(block.astype(F32)).astype(BF16)
    projected = jnp.dot(normed, proj_ref[...], preferred_element_type=F32)
    left = jax.nn.sigmoid(projected[:, 0:128]) * projected[:, 128:256]
    right = jax.nn.sigmoid(projected[:, 256:384]) * projected[:, 384:512]
    return left, right


def output_gate(block, gate_ref):
    normed = normalize(block.astype(F32)).astype(BF16)
    return jax.nn.sigmoid(jnp.dot(normed, gate_ref[...], preferred_element_type=F32))


def finish(block, summed, gate, final_ref):
    mixed = normalize(summed).astype(BF16)
    update = gate * jnp.dot(mixed, final_ref[...], preferred_element_type=F32)
    return (block.astype(F32) + update).astype(BF16)


def outer(a, b):
    a, b = a.astype(F32), b.astype(F32)
    i, j, k = 4, 8, a.shape[0] // 32
    a, b = a.reshape(i, k, 8, 128), b.reshape(j, k, 8, 128)
    total = None
    for n in range(k):
        term = a[:, None, n] * b[None, :, n]
        total = term if total is None else total + term
    return total


def kernel(
    map_in, proj1_in, gate1_in, final1_in, proj2_in, gate2_in, final2_in, out_ref,
    map_ref, proj1, gate1, final1, proj2, gate2, final2,
    send_z, send_l1, send_r1, left1, right1, send_p1, part1, own1, block1, middle,
    turned, send_l2, send_r2, left2, right2, send_p2, part2, block2,
    load, out_turn, out, in_turn, in_z, in_a_r1, in_b_r1, in_l1, in_p1, in_a_l2, in_b_l2, in_r2, in_p2, far,
):
    row, col = lax.axis_index("row"), lax.axis_index("col")
    y, zl, core = row // 8, row // 2 % 4, row % 2
    x, zh = col // 4, col % 4

    def at(x_, y_, zh_, zl_, core_):
        return (y_ * 8 + zl_ * 2 + core_, x_ * 4 + zh_)

    def plus(value, step):
        return (value + step) % 4

    def minus(value, step):
        return (value + 4 - step) % 4

    flat = x == y
    sibling = at(x, y, zh, zl, 1 - core)
    swapped = at(y, x, zh, zl, core)
    zl_sends, y_sends, x_sends, far_sends, near_sends = range(5)

    def copy(src, dst, send, recv, device):
        return pltpu.make_async_remote_copy(
            src_ref=src, dst_ref=dst, send_sem=send, recv_sem=recv, device_id=device, device_id_type=MESH
        )

    def push(src, dst, send, recv, device):
        copy(src, dst, send, recv, device).start()

    def push_unless(stays, src, dst, send, recv, device):
        @pl.when(jnp.logical_not(stays))
        def _():
            copy(src, dst, send, recv, device).start()

        @pl.when(stays)
        def _():
            pltpu.make_async_copy(src, dst, recv).start()

    def landed(like, recv):
        copy(like, like, out_turn.at[0], recv, sibling).wait_recv()

    def sent(like, send):
        copy(like, like, send, in_turn.at[0], sibling).wait_send()

    first_loads = [
        pltpu.make_async_copy(map_in, map_ref, load.at[0]),
        pltpu.make_async_copy(proj1_in, proj1, load.at[1]),
    ]
    later_loads = [
        pltpu.make_async_copy(src, dst, load.at[2])
        for src, dst in (
            (gate1_in, gate1), (final1_in, final1), (proj2_in, proj2), (gate2_in, gate2), (final2_in, final2),
        )
    ]

    barrier = pltpu.get_barrier_semaphore()
    greeted = []

    def greet(device, stays=None):
        def signal():
            pl.semaphore_signal(barrier, inc=1, device_id=device, device_id_type=MESH)

        if stays is None:
            signal()
            greeted.append(1)
        else:
            pl.when(jnp.logical_not(stays))(signal)
            greeted.append(1 - stays.astype(jnp.int32))

    for step in (2, 1, 3):
        if step != 2:
            greet(at(x, y, plus(zh, step), zl, core))
        for side in (0, 1):
            greet(at(x, plus(y, step), zh, zl, (core + side) % 2))
        greet(at(plus(x, step), y, zh, zl, core))
        greet(at(x, y, zh, plus(zl, step), core))
    greet(sibling)
    greet(swapped, flat)
    greet(at(y, x, zh, zl, 1 - core))

    for c in first_loads + later_loads:
        c.start()

    for c in first_loads:
        c.wait()
    left, right = prepare(map_ref[...].reshape(128, 128), proj1)
    columns = map_ref[...].astype(F32).reshape(8, 2, 8, 128)
    for side in range(2):
        send_z[side] = columns[:, side].reshape(64, 128).astype(BF16)
    send_r1[...] = right.astype(BF16)
    right1[x, zl] = send_r1[...]
    send_l1[...] = left.astype(BF16)

    pl.semaphore_wait(barrier, sum(greeted))

    for step in (1, 3):
        pl.semaphore_signal(far, inc=1, device_id=at(x, y, plus(zh, step), zl, core), device_id_type=MESH)
    push_unless(flat, send_l1, left1.at[2 * x + core], out_turn.at[0], in_turn.at[0], swapped)
    for step in (2, 1, 3):
        push(send_r1, right1.at[x, zl], out.at[0, zl_sends], in_a_r1.at[zl], at(x, y, zh, plus(zl, step), core))

    def right_over_x(from_zl):
        piece = right1.at[x, from_zl]
        for hop in (1, 3, 2):
            push(piece, piece, out.at[0, x_sends], in_b_r1.at[from_zl], at(plus(x, hop), y, zh, zl, core))

    piece = left1.at[2 * y + core]

    def left_over_y(side):
        for step in (1, 3, 2, 0):
            if step or side:
                push(piece, piece, out.at[0, y_sends], in_l1.at[side], at(x, plus(y, step), zh, zl, (core + side) % 2))

    def right_from(step):
        from_zl = plus(zh, step)

        @pl.when(from_zl != zl)
        def _():
            landed(right1.at[x, from_zl], in_a_r1.at[from_zl])
            right_over_x(from_zl)

    right_over_x(zl)
    landed(piece, in_turn.at[0])
    left_over_y(0)
    left_over_y(1)
    right_from(2)
    right_from(1)
    right_from(3)
    right_from(0)
    push_unless(flat, send_z.at[core], block1.at[core], out_turn.at[1], in_z.at[0], swapped)
    push(send_z.at[1 - core], block1.at[core], out.at[0, near_sends], in_z.at[0], at(y, x, zh, zl, 1 - core))

    for side in (0, 1):
        half = (core + side) % 2
        landed(left1.at[0 : 3 + side], in_l1.at[side])
        for step in (2, 1, 3, 0):
            to_zh = plus(zh, step)
            if side == 0:
                landed(right1.at[0, 0:3], in_b_r1.at[to_zh])

            def four_rows(quarter, _, step=step, to_zh=to_zh, half=half):
                total = None
                for from_x in range(4):
                    term = outer(
                        left1[2 * from_x + half, pl.ds(pl.multiple_of(quarter * 64, 64), 64), :], right1[from_x, to_zh]
                    )
                    total = term if total is None else total + term
                part = jnp.sum(total, axis=2).reshape(32, 128)
                rows = pl.ds(pl.multiple_of(quarter * 32, 32), 32)
                send_p1[2 * step + half, rows, :] = part.astype(BF16)
                if step == 0:
                    own1[half, rows, :] = part
                return 0

            lax.fori_loop(0, 2, four_rows, 0)
            if step == 2 and side == 0:
                pl.semaphore_wait(far, 2)
            if step:
                push(send_p1.at[2 * step + half], part1.at[2 * step + half], out.at[0, far_sends], in_p1,
                     at(x, y, to_zh, zl, core))

    landed(block1, in_z.at[0])
    pltpu.make_async_copy(left2.at[0:2], left2.at[0:2], load.at[2]).wait()
    block = block1[...].reshape(128, 128)
    gate = output_gate(block, gate1)
    landed(part1.at[0:6], in_p1)
    halves = [
        (own1[n] + part1[2 + n].astype(F32)) + (part1[4 + n].astype(F32) + part1[6 + n].astype(F32)) for n in range(2)
    ]
    summed = jnp.concatenate(halves, axis=0)
    block = finish(block, summed, gate, final1)
    middle[...] = block.reshape(2, 64, 128)

    left, right = prepare(block, proj2)
    turned[0] = left
    turned[1] = right
    for which, send_ref in ((0, send_l2), (1, send_r2)):
        for half in range(2):
            for j in range(0, 8, 2):
                pair = [turned[which, pl.ds(64 * half + j + k, 8, stride=8), :] for k in range(2)]
                send_ref[half, j * 8 : j * 8 + 16, :] = jnp.concatenate(pair, axis=0).astype(BF16)
    push_unless(flat, send_r2, right2.at[2 * x + core], out_turn.at[2], in_turn.at[1], swapped)
    left2[x, zh] = send_l2[...]
    for step in (2, 1, 3):
        push(send_l2, left2.at[x, zh], out.at[1, far_sends], in_a_l2.at[zh], at(x, y, plus(zh, step), zl, core))
    push_unless(flat, middle.at[core], block2.at[core], out_turn.at[3], in_z.at[1], swapped)
    push(middle.at[1 - core], block2.at[core], out.at[1, zl_sends], in_z.at[1], at(y, x, zh, zl, 1 - core))

    def left_over_x(step):
        from_zh = minus(zh, step)
        piece = left2.at[x, from_zh]
        if step:
            landed(piece, in_a_l2.at[from_zh])
        for hop in (1, 3, 2):
            push(piece, piece, out.at[1, x_sends], in_b_l2.at[from_zh], at(plus(x, hop), y, zh, zl, core))

    left_over_x(0)
    piece = right2.at[2 * y + core]
    landed(piece, in_turn.at[1])
    for step in (2, 1, 3, 0):
        for side in (1, 0):
            if step or side:
                push(piece, piece, out.at[1, y_sends], in_r2, at(x, plus(y, step), zh, zl, (core + side) % 2))
    left_over_x(1)
    left_over_x(3)
    left_over_x(2)
    landed(right2.at[0:7], in_r2)

    for step in (0, 1, 3, 2):
        from_zh = minus(zh, step)
        landed(left2.at[0, 0:3], in_b_l2.at[from_zh])

        def four_rows2(quarter, _, step=step, from_zh=from_zh):
            parts = []
            for j_half in range(2):
                total = None
                for from_x in range(4):
                    for other in range(2):
                        term = outer(
                            left2[from_x, from_zh, other, pl.ds(pl.multiple_of(quarter * 32, 32), 32), :],
                            right2[2 * from_x + j_half, other],
                        )
                        total = term if total is None else total + term
                parts.append(jnp.sum(total, axis=2).reshape(4, 1, 8, 128))
            send_p2[step, quarter] = jnp.concatenate(parts, axis=1).reshape(64, 128).astype(BF16)
            return 0

        for quarter in range(2):
            four_rows2(quarter, 0)
            push_unless(from_zh == zl, send_p2.at[step, quarter], part2.at[zl, quarter], out.at[1, near_sends], in_p2,
                        at(x, y, zh, from_zh, core))

    landed(block2, in_z.at[1])
    block = jnp.concatenate([block2[n].astype(F32).reshape(8, 1, 8, 128) for n in range(2)], axis=1).reshape(128, 128)
    gate = output_gate(block, gate2)
    landed(part2, in_p2)
    summed = [part2[n].astype(F32).reshape(128, 128) for n in range(4)]
    summed = (summed[0] + summed[1]) + (summed[2] + summed[3])
    out_ref[...] = finish(block, summed, gate, final2).reshape(8, 16, 128)

    sent(right1.at[0, 0:3], out.at[0, zl_sends])
    sent(left1.at[0:7], out.at[0, y_sends])
    sent(right1.at[0:3], out.at[0, x_sends])
    sent(send_p1.at[0:6], out.at[0, far_sends])
    sent(send_z.at[0], out.at[0, near_sends])
    sent(right2.at[0:7], out.at[1, y_sends])
    sent(left2.at[0:3], out.at[1, x_sends])
    sent(left2.at[0, 0:3], out.at[1, far_sends])
    sent(middle.at[0], out.at[1, zl_sends])
    sent(send_p2.at[0:3], out.at[1, near_sends])

    @pl.when(jnp.logical_not(flat))
    def _():
        sent(send_l1, out_turn.at[0])
        sent(block1.at[0], out_turn.at[1])
        sent(send_r2, out_turn.at[2])
        sent(block2.at[0], out_turn.at[3])


def body(*args):
    dma = pltpu.SemaphoreType.DMA
    weights = [pltpu.VMEM((128, 512), BF16), pltpu.VMEM((128, 128), BF16), pltpu.VMEM((128, 128), BF16)]
    tile = pltpu.VMEM((8, 16, 128), BF16)
    return pl.pallas_call(
        kernel,
        out_shape=jax.ShapeDtypeStruct((8, 16, 128), BF16),
        in_specs=[pl.BlockSpec(memory_space=pl.ANY)] * 7,
        out_specs=pl.BlockSpec(memory_space=pltpu.VMEM),
        scratch_shapes=[tile, *weights, *weights]
        + [pltpu.VMEM((2, 64, 128), BF16)]
        + [pltpu.VMEM((128, 128), BF16)] * 2
        + [pltpu.VMEM((8, 128, 128), BF16), pltpu.VMEM((4, 4, 128, 128), BF16)]
        + [pltpu.VMEM((8, 64, 128), BF16)] * 2
        + [pltpu.VMEM((2, 64, 128), F32)] + [pltpu.VMEM((2, 64, 128), BF16)] * 2
        + [pltpu.VMEM((2, 128, 128), F32)]
        + [pltpu.VMEM((2, 64, 128), BF16)] * 2
        + [pltpu.VMEM((4, 4, 2, 64, 128), BF16), pltpu.VMEM((8, 2, 64, 128), BF16)]
        + [pltpu.VMEM((4, 2, 64, 128), BF16)] * 2
        + [pltpu.VMEM((2, 64, 128), BF16)]
        + [dma((3,)), dma((4,)), dma((2, 5)), dma((2,)), dma((2,)), dma((4,)), dma((4,)), dma((2,)), dma]
        + [dma((4,)), dma((4,)), dma, dma, pltpu.SemaphoreType.REGULAR],
        compiler_params=pltpu.CompilerParams(
            collective_id=0, has_side_effects=True, vmem_limit_bytes=32 * 1024 * 1024
        ),
        name="triangles",
    )(*[pltpu.with_memory_space_constraint(a, pltpu.HBM) for a in args])


def solution(mesh):
    return jax.shard_map(
        body,
        mesh=mesh,
        in_specs=(P("row", "col", None), P(), P(), P(), P(), P(), P()),
        out_specs=P("row", "col", None),
        check_vma=False,
    )
```
